256 devices in a mesh: dp: 64 (over x, y, z_hi), tp: 4 (over z_lo, core).
Axes of the slice: x: 4, y: 4, z: 8 (z_hi: 4, z_lo: 2; z = z_hi * 2 + z_lo), core: 2. Of those that a mesh axis runs over, the one named last changes fastest.
Arguments:
- query_latent: bfloat16 [2, 128, 65536], P(None, 'dp', 'tp')
- query_rope: bfloat16 [2, 128, 8192], P(None, 'dp', 'tp'), may hold values from -6 to 6
- cache_latent: bfloat16 [128, 384, 512], P('dp')
- cache_rope: bfloat16 [128, 64, 384], P('dp'), may hold values from -6 to 6
- new_latent: bfloat16 [2, 128, 512], P(None, 'dp'), may hold values from -6 to 6
- new_rope: bfloat16 [2, 128, 64], P(None, 'dp'), may hold values from -6 to 6
- cache_lengths: int32 [128], P('dp'), may hold values from 2 to 384, as said below
- row_counts: int32 [64], replicated, may hold values from 1 to 2, as said below
- value_up: bfloat16 [128, 512, 128], P('tp'), may hold values from -0.25 to 0.25
- out_proj: bfloat16 [16384, 7168], P('tp', 'dp'), may hold values from -0.1875 to 0.1875
- norm_gain: float32 [7168], replicated, may hold values from 0.1 to 1.9
- expert_ids: int32 [2, 128, 4], replicated, may hold values from 0 to 15, all different within a row
- route_gates: float32 [2, 128, 4], replicated, may hold values from 0.1 to 1
- gate_proj: bfloat16 [7168, 32768], P(None, ('dp', 'tp')), may hold values from -0.0625 to 0.0625
- up_proj: bfloat16 [7168, 32768], P(None, ('dp', 'tp')), may hold values from -0.0625 to 0.0625
- down_proj: bfloat16 [32768, 7168], P(('dp', 'tp')), may hold values from -0.125 to 0.125
Outputs:
- hidden: bfloat16 [2, 128, 7168], P(None, None, 'dp')
- mixed: bfloat16 [2, 128, 7168], P(None, 'dp', 'tp')
The draws below stay inside these ranges and needn't reach their ends.
Inputs may be any that keep to these rules, and one draw needn't show every extreme that they name: `row_counts`: every replica has at least one live slot; in every draw some replica has all 2 slots live. `cache_lengths`: in every draw some slot uses all 384 positions.
All inputs are finite; a program needn't handle non-finite values.
Results may differ from the reference program's by a relative error of at most 0.014.
Values may be sent and summed in bfloat16 or wider, within the bound.
No kernel may reach another device: no remote copies, remote signals or barrier semaphores. Data moves between devices by JAX's collectives and lax.ppermute only.
A program may use at most 128 MiB of HBM per device.

```python
import math
import jax
import jax.numpy as jnp
from jax import lax

D = 7168
HEADS = 128
LAT = 512
ROPE = 64
HD = 128
FFN = 2048
EXPERTS = 16
TOPK = 4
STEPS = 2
SLOTS = 2
CACHE = 384
TOKENS = 128
N_DP = 64


def shared_latent(key):
    return jax.random.normal(jax.random.fold_in(key, 901), (TOKENS, LAT), jnp.float32)


def draw_cache_latent(key, part):
    first_rows = shared_latent(key)
    key = jax.random.fold_in(key, 11)
    base = jax.random.normal(key, (TOKENS, CACHE, LAT), jnp.float32)
    base = base.at[:, 0, :].set(first_rows)
    return base.astype(jnp.bfloat16)


def draw_query_latent(key, part):
    key = jax.random.fold_in(key, 12)
    base = jax.random.normal(key, (STEPS, TOKENS, HEADS, LAT), jnp.float32)
    return base.reshape(STEPS, TOKENS, HEADS * LAT).astype(jnp.bfloat16)


def draw_cache_lengths(key, part):
    key = jax.random.fold_in(key, 21)
    upper = jax.random.randint(jax.random.fold_in(key, 1), (TOKENS,), 2, CACHE + 1)
    chosen = jax.random.randint(jax.random.fold_in(key, 2), (TOKENS,), 2, upper + 1)
    where_full = jax.random.randint(jax.random.fold_in(key, 3), (), 0, TOKENS)
    return chosen.at[where_full].set(CACHE).astype(jnp.int32)


def draw_row_counts(key, part):
    key = jax.random.fold_in(key, 31)
    replicas = TOKENS // SLOTS
    upper = jax.random.randint(jax.random.fold_in(key, 1), (replicas,), 1, SLOTS + 1)
    chosen = jax.random.randint(jax.random.fold_in(key, 2), (replicas,), 1, upper + 1)
    where_full = jax.random.randint(jax.random.fold_in(key, 3), (), 0, replicas)
    return chosen.at[where_full].set(SLOTS).astype(jnp.int32)


def block_levels(rng, shape, shards, smallest, top_value):
    loudness = 1.0
    for axis_at, blocks in shards:
        draws = jax.random.uniform(jax.random.fold_in(jax.random.fold_in(rng, 6), axis_at), (blocks,), jnp.float32, smallest / len(shards), top_value / len(shards))
        loudness = loudness * jnp.repeat(jnp.exp(draws), shape[axis_at] // blocks).reshape((-1,) + (1,) * (len(shape) - 1 - axis_at))
    return loudness


def choose_distinct(stream_key, rows, count, top, lift):
    ranking = jax.random.permutation(jax.random.fold_in(stream_key, 1), count)
    favour = ranking
    for power in range(3):
        favour = favour * favour // count
    favour = favour * lift // count
    lots = jax.random.randint(jax.random.fold_in(stream_key, 2), (rows, count), 0, 4096) + favour
    fixed_rows = jax.random.permutation(jax.random.fold_in(stream_key, 3), rows)[jnp.arange(count) % rows]
    lots = jnp.where(jnp.arange(rows)[:, None] == fixed_rows[None, :], 1 << 14, lots)
    score = lots * count + jnp.arange(count)
    return lax.top_k(score.astype(jnp.int32), top)[1].astype(jnp.int32)


def scatter_about(key, extent, width, bound, pieces=(), held_as=jnp.bfloat16):
    entries = width * jax.random.normal(key, extent, jnp.float32)
    if pieces:
        entries = entries * block_levels(key, extent, pieces, -0.22, 0.18)
    return jnp.clip(entries, -bound, bound).astype(held_as)


def setup_inputs(seed: int = 0) -> dict:
    keys = jax.random.split(jax.random.key(seed), 17)
    return {
        "query_latent": draw_query_latent(jax.random.fold_in(keys[16], 71), 0),
        "query_rope": scatter_about(keys[1], (STEPS, TOKENS, HEADS * ROPE), 1.0, 6.0, ((1, 64), (2, 4))),
        "cache_latent": draw_cache_latent(jax.random.fold_in(keys[16], 71), 0),
        "cache_rope": scatter_about(keys[3], (TOKENS, ROPE, CACHE), 1.0, 6.0, ((0, 64),)),
        "new_latent": scatter_about(keys[4], (STEPS, TOKENS, LAT), 1.0, 6.0, ((1, 64),)),
        "new_rope": scatter_about(keys[5], (STEPS, TOKENS, ROPE), 1.0, 6.0, ((1, 64),)),
        "cache_lengths": draw_cache_lengths(jax.random.fold_in(keys[16], 71), 0),
        "row_counts": draw_row_counts(jax.random.fold_in(keys[16], 71), 0),
        "value_up": scatter_about(keys[8], (HEADS, LAT, HD), LAT ** -0.5, 0.25, ((0, 4),)),
        "out_proj": scatter_about(keys[9], (HEADS * HD, D), (HEADS * HD // 16) ** -0.5, 0.1875, ((0, 4), (1, 64))),
        "norm_gain": jnp.clip(1.0 + 0.18 * jax.random.normal(keys[10], (D,), jnp.float32), 0.1, 1.9),
        "expert_ids": choose_distinct(keys[11], STEPS * TOKENS, EXPERTS, TOPK, 4096).reshape((STEPS, TOKENS, TOPK)),
        "route_gates": jnp.clip(jnp.exp(jax.random.uniform(keys[12], (STEPS, TOKENS, TOPK), jnp.float32, math.log(0.1), math.log(1.0))), 0.1, 1.0),
        "gate_proj": scatter_about(keys[13], (D, EXPERTS * FFN), D ** -0.5, 0.0625, ((1, 256),)),
        "up_proj": scatter_about(keys[14], (D, EXPERTS * FFN), D ** -0.5, 0.0625, ((1, 256),)),
        "down_proj": scatter_about(keys[15], (EXPERTS * FFN, D), FFN ** -0.5, 0.125, ((0, 256),)),
    }


def attend_all(which_step, query_latent, query_rope, cache_latent, cache_rope, new_latent, new_rope, cache_lengths, live_rows, value_up):
    token_count = cache_latent.shape[0]
    scale_factor = (HD + ROPE) ** (-0.5)
    query_heads = query_latent[which_step].reshape(token_count, HEADS, LAT).astype(jnp.float32)
    rope_heads = query_rope[which_step].reshape(token_count, HEADS, ROPE).astype(jnp.float32)
    cache_values = cache_latent.astype(jnp.float32)
    cache_scores = jnp.einsum('thl,tcl->thc', query_heads, cache_values)
    cache_scores = (cache_scores + jnp.einsum('thr,trc->thc', rope_heads, cache_rope.astype(jnp.float32))) * scale_factor
    key_mask = jnp.arange(CACHE)[None, None, :] < cache_lengths[:, None, None]
    cache_scores = jnp.where(key_mask, cache_scores, -1e+30)
    fresh_latent = new_latent[:which_step + 1].astype(jnp.float32)
    fresh_rope = new_rope[:which_step + 1].astype(jnp.float32)
    new_scores = jnp.einsum('thl,ntl->thn', query_heads, fresh_latent)
    new_scores = (new_scores + jnp.einsum('thr,ntr->thn', rope_heads, fresh_rope)) * scale_factor
    all_scores = jnp.concatenate([cache_scores, new_scores], axis=2)
    top_score = lax.optimization_barrier(jnp.max(all_scores, axis=2, keepdims=True))
    expo = jnp.exp(all_scores - top_score)
    probs = (expo / lax.optimization_barrier(jnp.sum(expo, axis=2, keepdims=True))).astype(jnp.bfloat16).astype(jnp.float32)
    latent_context = jnp.einsum('thc,tcl->thl', probs[:, :, :CACHE], cache_values)
    latent_context = latent_context + jnp.einsum('thn,ntl->thl', probs[:, :, CACHE:], fresh_latent)
    latent_context = latent_context.astype(jnp.bfloat16).astype(jnp.float32)
    context_out = jnp.einsum('thl,hld->thd', latent_context, value_up.astype(jnp.float32)).astype(jnp.bfloat16)
    context_out = context_out.reshape(token_count, HEADS * HD)
    return jnp.where(live_rows[:, None], context_out, jnp.zeros_like(context_out))

def reference(query_latent, query_rope, cache_latent, cache_rope, new_latent, new_rope, cache_lengths, row_counts, value_up, out_proj, norm_gain, expert_ids, route_gates, gate_proj, up_proj, down_proj):
    token_count = SLOTS * N_DP
    live_rows = jnp.arange(token_count) % SLOTS < jnp.repeat(row_counts, SLOTS, total_repeat_length=token_count)
    live_float = live_rows.astype(jnp.float32)
    hidden_list = []
    mixed_list = []
    for which_step in range(STEPS):
        contexts = attend_all(which_step, query_latent, query_rope, cache_latent, cache_rope, new_latent, new_rope, cache_lengths, live_rows, value_up)
        hidden = jnp.dot(contexts, out_proj, preferred_element_type=jnp.float32).astype(jnp.bfloat16)
        row_values = hidden.astype(jnp.float32)
        normed = (row_values * lax.rsqrt(lax.optimization_barrier(jnp.mean(row_values * row_values, axis=1, keepdims=True)) + 1e-06) * norm_gain).astype(jnp.bfloat16)
        total = jnp.zeros((token_count, D), jnp.float32)
        for expert_id in range(EXPERTS):
            weight_col = lax.optimization_barrier(jnp.sum(jnp.where(expert_ids[which_step] == expert_id, route_gates[which_step], 0.0), axis=1)) * live_float
            low = expert_id * FFN
            gate_part = jnp.dot(normed, gate_proj[:, low:low + FFN], preferred_element_type=jnp.float32)
            up_part = jnp.dot(normed, up_proj[:, low:low + FFN], preferred_element_type=jnp.float32)
            inner = (jax.nn.silu(gate_part) * up_part * weight_col[:, None]).astype(jnp.bfloat16)
            total = total + jnp.dot(inner, down_proj[low:low + FFN, :], preferred_element_type=jnp.float32)
        hidden_list.append(hidden)
        mixed_list.append(total.astype(jnp.bfloat16))
    return (jnp.stack(hidden_list), jnp.stack(mixed_list))
```

```python
import jax
import jax.numpy as jnp
from jax import lax
from jax.sharding import Mesh, PartitionSpec as P

D = 7168
LAT = 512
ROPE = 64
HD = 128
FFN = 2048
STEPS = 2
SLOTS = 2
CACHE = 384

DP = ("x", "y", "h")
TP = ("l", "c")
XY = ("x", "y")
Z = ("h", "l")
NXY = 16
NZ = 8
NH = 4
TOK = 256
SWAP = ((0, 1), (1, 0))

bf16 = jnp.bfloat16
f32 = jnp.float32


def spread(value, axes, count):
    copies = jnp.broadcast_to(value[None], (count,) + value.shape)
    return lax.all_to_all(copies, axes, 0, 0)


def attend(query_latent, query_rope, cache_latent, cache_rope, new_latent, new_rope, cache_lengths, live, value_up):
    heads = value_up.shape[0]
    scale = (HD + ROPE) ** (-0.5)
    rows = STEPS * heads
    q = jnp.transpose(query_latent.reshape(STEPS, SLOTS, heads, LAT), (1, 0, 2, 3)).reshape(SLOTS, rows, LAT)
    qr = jnp.transpose(query_rope.reshape(STEPS, SLOTS, heads, ROPE), (1, 0, 2, 3)).reshape(SLOTS, rows, ROPE)
    old = jnp.einsum("bhl,bcl->bhc", q, cache_latent, preferred_element_type=f32)
    old = (old + jnp.einsum("bhr,brc->bhc", qr, cache_rope, preferred_element_type=f32)) * scale
    mask = jnp.arange(CACHE)[None, None, :] < cache_lengths[:, None, None]
    old = jnp.where(mask, old, -1e30)
    new = jnp.einsum("bhl,nbl->bhn", q, new_latent, preferred_element_type=f32)
    new = (new + jnp.einsum("bhr,nbr->bhn", qr, new_rope, preferred_element_type=f32)) * scale
    step_of_row = jnp.arange(rows)[:, None] // heads
    new = jnp.where((jnp.arange(STEPS)[None, :] <= step_of_row)[None], new, -1e30)
    top = jnp.maximum(jnp.max(old, axis=2, keepdims=True), jnp.max(new, axis=2, keepdims=True))
    eo = jnp.exp(old - top)
    en = jnp.exp(new - top)
    total = jnp.sum(eo, axis=2, keepdims=True) + jnp.sum(en, axis=2, keepdims=True)
    po = (eo / total).astype(bf16)
    pn = (en / total).astype(bf16)
    lat = jnp.einsum("bhc,bcl->bhl", po, cache_latent, preferred_element_type=f32)
    lat = lat + jnp.einsum("bhn,nbl->bhl", pn, new_latent, preferred_element_type=f32)
    lat = lat.astype(bf16).reshape(SLOTS, STEPS, heads, LAT)
    ctx = jnp.einsum("bshl,hld->sbhd", lat, value_up, preferred_element_type=f32).astype(bf16)
    ctx = jnp.where(live[None, :, None, None], ctx, jnp.zeros_like(ctx))
    return ctx.reshape(STEPS * SLOTS, heads * HD)


def body(
    query_latent,
    query_rope,
    cache_latent,
    cache_rope,
    new_latent,
    new_rope,
    cache_lengths,
    row_counts,
    value_up,
    out_proj,
    norm_gain,
    expert_ids,
    route_gates,
    gate_proj,
    up_proj,
    down_proj,
):
    replica = lax.axis_index(DP)
    core = lax.axis_index("c")
    own_count = lax.dynamic_slice_in_dim(row_counts, replica, 1, 0)
    live = jnp.arange(SLOTS) < own_count

    down = down_proj.reshape(128, 2, 2, D // 4)
    down_keep = lax.dynamic_index_in_dim(down, core, 2, keepdims=False)
    down_send = lax.dynamic_index_in_dim(down, 1 - core, 2, keepdims=False)
    down_got = lax.ppermute(down_send, "c", SWAP)
    down_both = jnp.concatenate([down_keep, down_got], axis=0).reshape(256, D // 2)

    ctx = attend(
        query_latent, query_rope, cache_latent, cache_rope, new_latent, new_rope, cache_lengths, live, value_up
    )
    ctx = spread(ctx, "h", NH).reshape(NH * STEPS * SLOTS, -1)
    ctx = spread(ctx, XY, NXY).reshape(TOK, -1)

    part = jnp.dot(ctx, out_proj, preferred_element_type=f32).T
    keep = lax.dynamic_slice_in_dim(part, core * 128, 128, 1)
    send = lax.dynamic_slice_in_dim(part, (1 - core) * 128, 128, 1)
    chip = (keep + lax.ppermute(send, "c", SWAP)).astype(bf16)
    pieces = spread(chip, Z, NZ).reshape(NH, 2, D // 64, 128).astype(f32)
    hid = jnp.sum(pieces, axis=1)
    hid_b = hid.astype(bf16)

    own_hid = lax.dynamic_index_in_dim(hid_b, lax.axis_index("h"), 0, keepdims=False)
    other_hid = lax.ppermute(own_hid, "c", SWAP)
    first = jnp.where(core == 0, own_hid, other_hid)
    second = jnp.where(core == 0, other_hid, own_hid)
    hidden = jnp.concatenate([first, second], axis=1).T.reshape(64, STEPS, SLOTS, D // 64)
    hidden = jnp.transpose(hidden, (1, 0, 2, 3)).reshape(STEPS, 128, D // 64)

    hid_f = hid_b.astype(f32).reshape(D // 16, 128)
    column = lax.axis_index(XY)
    gain = lax.dynamic_slice_in_dim(norm_gain, column * (D // 16), D // 16, 0)
    scaled = (hid_f * gain[:, None]).astype(bf16)
    squares = jnp.sum(hid_f * hid_f, axis=0, keepdims=True)
    high = squares.astype(bf16)
    low = (squares - high.astype(f32)).astype(bf16)
    packed = jnp.concatenate([scaled, high, low, jnp.zeros((14, 128), bf16)], axis=0)
    rows_half = spread(packed, XY, NXY)
    rows_other = lax.ppermute(rows_half, "c", SWAP)

    expert = column
    fours = jnp.sum(jnp.where(expert_ids == expert, route_gates, 0.0), axis=2)
    live_rows = (jnp.arange(SLOTS)[None, :] < row_counts[:, None]).astype(f32)
    weight = fours.reshape(STEPS, 64, SLOTS) * live_rows[None]
    weight = jnp.transpose(weight, (1, 0, 2)).reshape(2, 128)

    def experts(rows, scale):
        total = jnp.sum(rows[:, 448:450, :].astype(f32), axis=(0, 1))
        inv = lax.rsqrt(total / D + 1e-06)
        wide = rows[:, :448, :].reshape(D, 128)
        gate = lax.dot_general(gate_proj, wide, (((0,), (0,)), ((), ())), preferred_element_type=f32) * inv
        up = lax.dot_general(up_proj, wide, (((0,), (0,)), ((), ())), preferred_element_type=f32) * inv
        return (jax.nn.silu(gate) * up * scale).astype(bf16)

    inner_a = experts(rows_half, lax.dynamic_index_in_dim(weight, core, 0, keepdims=False))
    inner_b = experts(rows_other, lax.dynamic_index_in_dim(weight, 1 - core, 0, keepdims=False))
    got_a = lax.ppermute(inner_a, "c", SWAP)
    got_b = lax.ppermute(inner_b, "c", SWAP)
    mine = jnp.concatenate([inner_a, got_b], axis=0)
    theirs = jnp.concatenate([inner_b, got_a], axis=0)
    first = jnp.where(core == 0, mine, theirs)
    second = jnp.where(core == 0, theirs, mine)
    inner = jnp.concatenate([first, second], axis=1)

    wide = lax.dot_general(inner, down_both, (((0,), (0,)), ((), ())), preferred_element_type=f32).astype(bf16)
    got = lax.all_to_all(wide.reshape(NXY, 16, D // 2), XY, 0, 0)
    column_sum = jnp.sum(got.astype(f32), axis=0).astype(bf16)
    column_sum = jnp.transpose(column_sum.reshape(NH, 4, 2, D // 4), (0, 2, 1, 3)).reshape(NZ, 4, D // 4)
    own = jnp.sum(lax.all_to_all(column_sum, Z, 0, 0).astype(f32), axis=0)
    mixed = own.astype(bf16).reshape(STEPS, SLOTS, D // 4)
    return hidden, mixed


def solution(mesh):
    fine = Mesh(mesh.devices.reshape(4, 4, 4, 2, 2), ("x", "y", "h", "l", "c"))
    return jax.shard_map(
        body,
        mesh=fine,
        in_specs=(
            P(None, DP, TP),
            P(None, DP, TP),
            P(DP, None, None),
            P(DP, None, None),
            P(None, DP, None),
            P(None, DP, None),
            P(DP),
            P(),
            P(TP, None, None),
            P(TP, DP),
            P(),
            P(),
            P(),
            P(None, DP + TP),
            P(None, DP + TP),
            P(DP + TP, None),
        ),
        out_specs=(P(None, None, DP), P(None, DP, TP)),
        check_vma=False,
    )
```

```python
import jax
import jax.numpy as jnp
from jax import lax
from jax.sharding import Mesh, PartitionSpec as P

D = 7168
LAT = 512
ROPE = 64
HD = 128
FFN = 2048
STEPS = 2
SLOTS = 2
CACHE = 384

DP = ("x", "y", "h")
TP = ("l", "c")
XY = ("x", "y")
Z = ("h", "l")
NXY = 16
NZ = 8
NH = 4
TOK = 256
SWAP = ((0, 1), (1, 0))

bf16 = jnp.bfloat16
f32 = jnp.float32


def spread(value, axes, count):
    copies = jnp.broadcast_to(value[None], (count,) + value.shape)
    return lax.all_to_all(copies, axes, 0, 0)


def attend(query_latent, query_rope, cache_latent, cache_rope, new_latent, new_rope, cache_lengths, live, value_up):
    heads = value_up.shape[0]
    scale = (HD + ROPE) ** (-0.5)
    rows = STEPS * heads
    q = jnp.transpose(query_latent.reshape(STEPS, SLOTS, heads, LAT), (1, 0, 2, 3)).reshape(SLOTS, rows, LAT)
    qr = jnp.transpose(query_rope.reshape(STEPS, SLOTS, heads, ROPE), (1, 0, 2, 3)).reshape(SLOTS, rows, ROPE)
    old = jnp.einsum("bhl,bcl->bhc", q, cache_latent, preferred_element_type=f32)
    old = (old + jnp.einsum("bhr,brc->bhc", qr, cache_rope, preferred_element_type=f32)) * scale
    mask = jnp.arange(CACHE)[None, None, :] < cache_lengths[:, None, None]
    old = jnp.where(mask, old, -1e30)
    new = jnp.einsum("bhl,nbl->bhn", q, new_latent, preferred_element_type=f32)
    new = (new + jnp.einsum("bhr,nbr->bhn", qr, new_rope, preferred_element_type=f32)) * scale
    step_of_row = jnp.arange(rows)[:, None] // heads
    new = jnp.where((jnp.arange(STEPS)[None, :] <= step_of_row)[None], new, -1e30)
    top = jnp.maximum(jnp.max(old, axis=2, keepdims=True), jnp.max(new, axis=2, keepdims=True))
    eo = jnp.exp(old - top)
    en = jnp.exp(new - top)
    total = jnp.sum(eo, axis=2, keepdims=True) + jnp.sum(en, axis=2, keepdims=True)
    po = (eo / total).astype(bf16)
    pn = (en / total).astype(bf16)
    lat = jnp.einsum("bhc,bcl->bhl", po, cache_latent, preferred_element_type=f32)
    lat = lat + jnp.einsum("bhn,nbl->bhl", pn, new_latent, preferred_element_type=f32)
    lat = lat.astype(bf16).reshape(SLOTS, STEPS, heads, LAT)
    ctx = jnp.einsum("bshl,hld->sbhd", lat, value_up, preferred_element_type=f32).astype(bf16)
    ctx = jnp.where(live[None, :, None, None], ctx, jnp.zeros_like(ctx))
    return ctx.reshape(STEPS * SLOTS, heads * HD)


def body(
    query_latent,
    query_rope,
    cache_latent,
    cache_rope,
    new_latent,
    new_rope,
    cache_lengths,
    row_counts,
    value_up,
    out_proj,
    norm_gain,
    expert_ids,
    route_gates,
    gate_proj,
    up_proj,
    down_proj,
):
    replica = lax.axis_index(DP)
    core = lax.axis_index("c")
    column = lax.axis_index(XY)
    own_count = lax.dynamic_slice_in_dim(row_counts, replica, 1, 0)
    live = jnp.arange(SLOTS) < own_count

    gate_other = lax.ppermute(gate_proj, "c", SWAP)
    up_other = lax.ppermute(up_proj, "c", SWAP)
    down_other = lax.ppermute(down_proj, "c", SWAP)

    ctx = attend(
        query_latent, query_rope, cache_latent, cache_rope, new_latent, new_rope, cache_lengths, live, value_up
    )
    gain = lax.dynamic_slice_in_dim(norm_gain, column * (D // 16), D // 16, 0)
    gain = jnp.broadcast_to(gain[:, None], (D // 16, 128))
    fours = jnp.sum(jnp.where(expert_ids == column, route_gates, 0.0), axis=2)
    live_rows = (jnp.arange(SLOTS)[None, :] < row_counts[:, None]).astype(f32).reshape(128)
    weight = lax.dynamic_index_in_dim(fours, core, 0, keepdims=False) * live_rows
    ctx, gain, weight = lax.optimization_barrier((ctx, gain, weight))

    ctx = spread(ctx, "h", NH).reshape(NH, STEPS, SLOTS, -1)
    ctx = jnp.transpose(ctx, (1, 0, 2, 3)).reshape(16, -1)
    ctx = spread(ctx, XY, NXY).reshape(TOK, -1)

    part = jnp.dot(ctx, out_proj, preferred_element_type=f32).reshape(NXY, STEPS, 8, D // 64)
    keep = lax.dynamic_index_in_dim(part, core, 1, keepdims=False).reshape(128, D // 64).T
    send = lax.dynamic_index_in_dim(part, 1 - core, 1, keepdims=False).reshape(128, D // 64).T
    chip = (keep + lax.ppermute(send, "c", SWAP)).astype(bf16)
    pieces = spread(chip, Z, NZ).reshape(NH, 2, D // 64, 128).astype(f32)
    hid = jnp.sum(pieces, axis=1).astype(bf16)
    own_hid = lax.dynamic_index_in_dim(hid, lax.axis_index("h"), 0, keepdims=False)

    hid_f = hid.astype(f32).reshape(D // 16, 128)
    scaled = (hid_f * gain).astype(bf16)
    squares = jnp.sum(hid_f * hid_f, axis=0, keepdims=True)
    high = squares.astype(bf16)
    low = (squares - high.astype(f32)).astype(bf16)
    packed = jnp.concatenate([scaled, high, low, jnp.zeros((14, 128), bf16)], axis=0)
    packed, own_hid = lax.optimization_barrier((packed, own_hid))
    rows = spread(packed, XY, NXY)

    rows, own_hid = lax.optimization_barrier((rows, own_hid))
    total = jnp.sum(rows[:, 448:450, :].astype(f32), axis=(0, 1))
    inv = lax.rsqrt(total / D + 1e-06)
    wide = rows[:, :448, :].reshape(D, 128)

    def product(weights):
        return lax.dot_general(weights, wide, (((0,), (0,)), ((), ())), preferred_element_type=f32) * inv

    inner = [
        (jax.nn.silu(product(gate)) * product(up) * weight).astype(bf16)
        for gate, up in ((gate_proj, up_proj), (gate_other, up_other))
    ]
    inner = jnp.concatenate(inner, axis=0)
    down = jnp.concatenate([down_proj, down_other], axis=0)
    out = lax.dot_general(inner, down, (((0,), (0,)), ((), ())), preferred_element_type=f32).astype(bf16)

    other_hid = lax.ppermute(own_hid, "c", SWAP)
    steps = jnp.where(core == 0, jnp.stack([own_hid, other_hid]), jnp.stack([other_hid, own_hid]))
    hidden = jnp.transpose(steps, (0, 2, 1))

    out, hidden = lax.optimization_barrier((out, hidden))
    got = lax.all_to_all(out.reshape(NXY, 8, D), XY, 0, 0)
    got, hidden = lax.optimization_barrier((got, hidden))
    sums = jnp.sum(got.astype(f32), axis=0).astype(bf16)
    sums = jnp.transpose(sums.reshape(NH, SLOTS, 4, D // 4), (0, 2, 1, 3)).reshape(16, SLOTS, D // 4)
    own = lax.all_to_all(sums, ("h", "l", "c"), 0, 0)
    mixed = jnp.sum(own.astype(f32).reshape(NZ, STEPS, SLOTS, D // 4), axis=0).astype(bf16)
    return hidden, mixed


def solution(mesh):
    fine = Mesh(mesh.devices.reshape(4, 4, 4, 2, 2), ("x", "y", "h", "l", "c"))
    return jax.shard_map(
        body,
        mesh=fine,
        in_specs=(
            P(None, DP, TP),
            P(None, DP, TP),
            P(DP, None, None),
            P(DP, None, None),
            P(None, DP, None),
            P(None, DP, None),
            P(DP),
            P(),
            P(TP, None, None),
            P(TP, DP),
            P(),
            P(),
            P(),
            P(None, DP + TP),
            P(None, DP + TP),
            P(DP + TP, None),
        ),
        out_specs=(P(None, None, DP), P(None, DP, TP)),
        check_vma=False,
    )
```

```python
import jax
import jax.numpy as jnp
from jax import lax
from jax.experimental import pallas as pl
from jax.experimental.pallas import tpu as pltpu
from jax.sharding import Mesh, PartitionSpec as P

D = 7168
LAT = 512
ROPE = 64
HD = 128
FFN = 2048
STEPS = 2
SLOTS = 2
CACHE = 384

DP = ("x", "y", "h")
TP = ("l", "c")
XY = ("x", "y")
Z = ("h", "l")
NXY = 16
NZ = 8
NH = 4
SWAP = ((0, 1), (1, 0))

bf16 = jnp.bfloat16
f32 = jnp.float32


def spread(value, axes, count):
    copies = jnp.broadcast_to(value[None], (count,) + value.shape)
    return lax.all_to_all(copies, axes, 0, 0)


def attend(query_latent, query_rope, cache_latent, cache_rope, new_latent, new_rope, cache_lengths, live, value_up):
    heads = value_up.shape[0]
    scale = (HD + ROPE) ** (-0.5)
    rows = STEPS * heads
    q = jnp.transpose(query_latent.reshape(STEPS, SLOTS, heads, LAT), (1, 0, 2, 3)).reshape(SLOTS, rows, LAT)
    qr = jnp.transpose(query_rope.reshape(STEPS, SLOTS, heads, ROPE), (1, 0, 2, 3)).reshape(SLOTS, rows, ROPE)
    old = jnp.einsum("bhl,bcl->bhc", q, cache_latent, preferred_element_type=f32)
    old = (old + jnp.einsum("bhr,brc->bhc", qr, cache_rope, preferred_element_type=f32)) * scale
    mask = jnp.arange(CACHE)[None, None, :] < cache_lengths[:, None, None]
    old = jnp.where(mask, old, -1e30)
    new = jnp.einsum("bhl,nbl->bhn", q, new_latent, preferred_element_type=f32)
    new = (new + jnp.einsum("bhr,nbr->bhn", qr, new_rope, preferred_element_type=f32)) * scale
    step_of_row = jnp.arange(rows)[:, None] // heads
    new = jnp.where((jnp.arange(STEPS)[None, :] <= step_of_row)[None], new, -1e30)
    top = jnp.maximum(jnp.max(old, axis=2, keepdims=True), jnp.max(new, axis=2, keepdims=True))
    eo = jnp.exp(old - top)
    en = jnp.exp(new - top)
    total = jnp.sum(eo, axis=2, keepdims=True) + jnp.sum(en, axis=2, keepdims=True)
    po = (eo / total).astype(bf16)
    pn = (en / total).astype(bf16)
    lat = jnp.einsum("bhc,bcl->bhl", po, cache_latent, preferred_element_type=f32)
    lat = lat + jnp.einsum("bhn,nbl->bhl", pn, new_latent, preferred_element_type=f32)
    lat = lat.astype(bf16).reshape(SLOTS, STEPS, heads, LAT)
    ctx = jnp.einsum("bshl,hld->sbhd", lat, value_up, preferred_element_type=f32).astype(bf16)
    ctx = jnp.where(live[None, :, None, None], ctx, jnp.zeros_like(ctx))
    return ctx.reshape(STEPS * SLOTS, heads * HD)


PARTS = 4


def experts_kernel(rows, weight, g0, g1, u0, u1, d0, d1, out, acc, tot, inner):
    step = pl.program_id(0)

    @pl.when(step == 0)
    def _():
        acc[...] = jnp.zeros_like(acc)
        tot[...] = jnp.zeros_like(tot)

    @pl.when(step < PARTS)
    def _():
        wide = rows[:, : D // 16, :].reshape(D // PARTS, 128)
        for j, w in enumerate((g0, u0, g1, u1)):
            acc[j] += lax.dot_general(w[...], wide, (((0,), (0,)), ((), ())), preferred_element_type=f32)
        tot[...] += jnp.sum(rows[:, D // 16 :, :].astype(f32), axis=(0, 1))[None]

    @pl.when(step == PARTS - 1)
    def _():
        inv = lax.rsqrt(tot[...] / D + 1e-06)
        for j in range(2):
            gate = acc[2 * j] * inv
            up = acc[2 * j + 1] * inv
            act = gate / (1.0 + jnp.exp(-gate))
            inner[j] = (act * up * weight[...]).astype(bf16)

    @pl.when(step >= PARTS)
    def _():
        dims = (((0,), (0,)), ((), ()))
        res = lax.dot_general(inner[0], d0[...], dims, preferred_element_type=f32)
        res += lax.dot_general(inner[1], d1[...], dims, preferred_element_type=f32)
        out[...] = res.astype(bf16)


def experts(rows, weight, *weights):
    first = lambda i: jnp.minimum(i, PARTS - 1)
    last = lambda i: jnp.maximum(i - PARTS, 0)
    k_spec = pl.BlockSpec((D // PARTS, 128), lambda i: (first(i), 0))
    n_spec = pl.BlockSpec((128, D // PARTS), lambda i: (0, last(i)))
    return pl.pallas_call(
        experts_kernel,
        grid=(2 * PARTS,),
        in_specs=[
            pl.BlockSpec((NXY // PARTS, D // 16 + 16, 128), lambda i: (first(i), 0, 0)),
            pl.BlockSpec((1, 128), lambda i: (0, 0)),
            k_spec,
            k_spec,
            k_spec,
            k_spec,
            n_spec,
            n_spec,
        ],
        out_specs=pl.BlockSpec((128, D // PARTS), lambda i: (0, last(i))),
        out_shape=jax.ShapeDtypeStruct((128, D), bf16),
        scratch_shapes=[
            pltpu.VMEM((4, 128, 128), f32),
            pltpu.VMEM((1, 128), f32),
            pltpu.VMEM((2, 128, 128), bf16),
        ],
        compiler_params=pltpu.CompilerParams(vmem_limit_bytes=24 * 1024 * 1024),
        cost_estimate=pl.CostEstimate(flops=705_000_000, bytes_accessed=15_000_000, transcendentals=32768),
    )(rows, weight, *weights)


def body(
    query_latent,
    query_rope,
    cache_latent,
    cache_rope,
    new_latent,
    new_rope,
    cache_lengths,
    row_counts,
    value_up,
    out_proj,
    norm_gain,
    expert_ids,
    route_gates,
    gate_proj,
    up_proj,
    down_proj,
):
    replica = lax.axis_index(DP)
    core = lax.axis_index("c")
    column = lax.axis_index(XY)
    own_count = lax.dynamic_slice_in_dim(row_counts, replica, 1, 0)
    live = jnp.arange(SLOTS) < own_count

    out_other = lax.ppermute(out_proj, "c", SWAP)
    gate_other = lax.ppermute(gate_proj, "c", SWAP)
    up_other = lax.ppermute(up_proj, "c", SWAP)
    down_other = lax.ppermute(down_proj, "c", SWAP)

    ctx = attend(
        query_latent, query_rope, cache_latent, cache_rope, new_latent, new_rope, cache_lengths, live, value_up
    ).reshape(STEPS, SLOTS, -1)
    ctx_keep = lax.dynamic_index_in_dim(ctx, core, 0, keepdims=False)
    ctx_send = lax.dynamic_index_in_dim(ctx, 1 - core, 0, keepdims=False)
    ctx = jnp.concatenate([ctx_keep, lax.ppermute(ctx_send, "c", SWAP)], axis=1)
    gain = lax.dynamic_slice_in_dim(norm_gain, column * (D // 16), D // 16, 0)
    gain = jnp.broadcast_to(gain[:, None], (D // 16, 128))
    fours = jnp.sum(jnp.where(expert_ids == column, route_gates, 0.0), axis=2)
    live_rows = (jnp.arange(SLOTS)[None, :] < row_counts[:, None]).astype(f32).reshape(128)
    weight = lax.dynamic_index_in_dim(fours, core, 0, keepdims=False) * live_rows
    weight = weight[None]
    ctx, gain, weight = lax.optimization_barrier((ctx, gain, weight))

    ctx = spread(ctx, "h", NH).reshape(8, -1)
    ctx, out_other, gate_other, up_other, down_other = lax.optimization_barrier(
        (ctx, out_other, gate_other, up_other, down_other)
    )
    ctx = spread(ctx, XY, NXY).reshape(128, -1)

    half = ctx.shape[1] // 2
    part = jnp.dot(ctx[:, :half], out_proj, preferred_element_type=f32)
    part = part + jnp.dot(ctx[:, half:], out_other, preferred_element_type=f32)
    chip = part.T.astype(bf16)
    pieces = spread(chip, Z, NZ).reshape(NH, 2, D // 64, 128).astype(f32)
    hid = jnp.sum(pieces, axis=1).astype(bf16)
    own_hid = lax.dynamic_index_in_dim(hid, lax.axis_index("h"), 0, keepdims=False)

    hid_f = hid.astype(f32).reshape(D // 16, 128)
    scaled = (hid_f * gain).astype(bf16)
    squares = jnp.sum(hid_f * hid_f, axis=0, keepdims=True)
    high = squares.astype(bf16)
    low = (squares - high.astype(f32)).astype(bf16)
    packed = jnp.concatenate([scaled, high, low, jnp.zeros((14, 128), bf16)], axis=0)
    packed, own_hid = lax.optimization_barrier((packed, own_hid))
    rows = spread(packed, XY, NXY)
    rows, own_hid = lax.optimization_barrier((rows, own_hid))

    out = experts(rows, weight, gate_proj, gate_other, up_proj, up_other, down_proj, down_other)
    out, own_hid = lax.optimization_barrier((out, own_hid))
    got = lax.all_to_all(out.reshape(NXY, 8, D), XY, 0, 0)
    got, own_hid = lax.optimization_barrier((got, own_hid))
    sums = jnp.sum(got.astype(f32), axis=0).astype(bf16)
    sums = jnp.transpose(sums.reshape(NH, SLOTS, 4, D // 4), (0, 2, 1, 3)).reshape(16, SLOTS, D // 4)

    other_hid = lax.ppermute(own_hid, "c", SWAP)
    steps = jnp.where(core == 0, jnp.stack([own_hid, other_hid]), jnp.stack([other_hid, own_hid]))
    hidden = jnp.transpose(steps, (0, 2, 1))

    own = lax.all_to_all(sums, ("h", "l", "c"), 0, 0)
    mixed = jnp.sum(own.astype(f32).reshape(NZ, STEPS, SLOTS, D // 4), axis=0).astype(bf16)
    return hidden, mixed


def solution(mesh):
    fine = Mesh(mesh.devices.reshape(4, 4, 4, 2, 2), ("x", "y", "h", "l", "c"))
    return jax.shard_map(
        body,
        mesh=fine,
        in_specs=(
            P(None, DP, TP),
            P(None, DP, TP),
            P(DP, None, None),
            P(DP, None, None),
            P(None, DP, None),
            P(None, DP, None),
            P(DP),
            P(),
            P(TP, None, None),
            P(TP, DP),
            P(),
            P(),
            P(),
            P(None, DP + TP),
            P(None, DP + TP),
            P(DP + TP, None),
        ),
        out_specs=(P(None, None, DP), P(None, DP, TP)),
        check_vma=False,
    )
```

```python
import jax
import jax.numpy as jnp
from jax import lax
from jax.experimental import pallas as pl
from jax.experimental.pallas import tpu as pltpu
from jax.sharding import Mesh, PartitionSpec as P

D = 7168
LAT = 512
ROPE = 64
HD = 128
FFN = 2048
STEPS = 2
SLOTS = 2
CACHE = 384

DP = ("x", "y", "h")
TP = ("l", "c")
XY = ("x", "y")
Z = ("h", "l")
NXY = 16
NZ = 8
NH = 4
SWAP = ((0, 1), (1, 0))

bf16 = jnp.bfloat16
f32 = jnp.float32


def spread(value, axes, count):
    copies = jnp.broadcast_to(value[None], (count,) + value.shape)
    return lax.all_to_all(copies, axes, 0, 0)


def attend_kernel(place, lengths, counts, ql_hbm, qr_hbm, cl_hbm, cr_hbm, nl_hbm, nr_hbm, v_hbm, out,
                  ql, qr, cl, cr, nl, nr, v, q_rows, r_rows, lat, sems):
    pairs = ((ql_hbm, ql), (qr_hbm, qr), (cl_hbm, cl), (cr_hbm, cr), (nl_hbm, nl), (nr_hbm, nr), (v_hbm, v))
    copies = [pltpu.make_async_copy(src, dst, sems.at[i]) for i, (src, dst) in enumerate(pairs)]
    for copy in copies:
        copy.start()
    heads = v.shape[0]
    rows = STEPS * heads
    scale = (HD + ROPE) ** (-0.5)
    copies[0].wait()
    copies[1].wait()
    for s in range(STEPS):
        for h in range(heads):
            q_rows[:, s * heads + h, :] = ql[s, :, h * LAT : (h + 1) * LAT].astype(f32)
        for p in range(heads // 2):
            pair = qr[s, :, p * 2 * ROPE : (p + 1) * 2 * ROPE].astype(f32)
            r_rows[:, s * heads + 2 * p, :] = pair
            r_rows[:, s * heads + 2 * p + 1, :] = pair
    for copy in copies[2:6]:
        copy.wait()
    step_of_row = lax.broadcasted_iota(jnp.int32, (rows, 1), 0) // heads
    position = lax.broadcasted_iota(jnp.int32, (rows, CACHE), 1)
    row_id = lax.broadcasted_iota(jnp.int32, (rows, 2 * ROPE), 0)
    lane_id = lax.broadcasted_iota(jnp.int32, (rows, 2 * ROPE), 1)
    own_half = row_id % 2 == lane_id // ROPE
    dims = (((1,), (1,)), ((), ()))
    for b in range(SLOTS):
        qf = q_rows[b]
        rf = jnp.where(own_half, r_rows[b], 0.0)
        rope = jnp.concatenate([cr[b], cr[b]], axis=0)
        old = lax.dot_general(qf.astype(bf16), cl[b], dims, preferred_element_type=f32)
        old = (old + jnp.dot(rf.astype(bf16), rope, preferred_element_type=f32)) * scale
        old = jnp.where(position < lengths[b], old, -1e30)
        top = jnp.max(old, axis=1, keepdims=True)
        new = []
        for i in range(STEPS):
            fresh_rope = nr[i, b : b + 1, :].astype(f32)
            n = jnp.sum(qf * nl[i, b : b + 1, :].astype(f32), axis=1, keepdims=True)
            n += jnp.sum(rf * jnp.concatenate([fresh_rope, fresh_rope], axis=1), axis=1, keepdims=True)
            n = jnp.where(step_of_row >= i, n * scale, -1e30)
            new.append(n)
            top = jnp.maximum(top, n)
        old = jnp.exp(old - top)
        new = [jnp.exp(n - top) for n in new]
        total = jnp.sum(old, axis=1, keepdims=True) + new[0] + new[1]
        res = jnp.dot((old / total).astype(bf16), cl[b], preferred_element_type=f32)
        for i in range(STEPS):
            res += (new[i] / total).astype(bf16).astype(f32) * nl[i, b : b + 1, :].astype(f32)
        for s in range(STEPS):
            lat[:, s * SLOTS + b, :] = res[s * heads : (s + 1) * heads, :]
    copies[6].wait()
    slot = lax.broadcasted_iota(jnp.int32, (STEPS * SLOTS, HD), 0) % SLOTS
    live = slot < counts[place[0]]
    for h in range(heads):
        ctx = jnp.dot(lat[h].astype(bf16), v[h], preferred_element_type=f32)
        out[:, h * HD : (h + 1) * HD] = jnp.where(live, ctx[: STEPS * SLOTS], 0.0).astype(bf16)


def attend(place, lengths, counts, *arrays):
    heads = arrays[-1].shape[0]
    scalars = pl.BlockSpec(memory_space=pltpu.SMEM)
    far = pl.BlockSpec(memory_space=pl.ANY)
    return pl.pallas_call(
        attend_kernel,
        in_specs=[scalars] * 3 + [far] * 7,
        out_specs=pl.BlockSpec(memory_space=pltpu.VMEM),
        out_shape=jax.ShapeDtypeStruct((STEPS * SLOTS, heads * HD), bf16),
        scratch_shapes=[pltpu.VMEM(a.shape, bf16) for a in arrays]
        + [
            pltpu.VMEM((SLOTS, STEPS * heads, LAT), f32),
            pltpu.VMEM((SLOTS, STEPS * heads, 2 * ROPE), f32),
            pltpu.VMEM((heads, 8, LAT), f32),
            pltpu.SemaphoreType.DMA((7,)),
        ],
        compiler_params=pltpu.CompilerParams(vmem_limit_bytes=52 * 1024 * 1024),
        cost_estimate=pl.CostEstimate(flops=160_000_000, bytes_accessed=6_000_000, transcendentals=50_000),
    )(place, lengths, counts, *arrays)


def experts_kernel(rows, weight, g0, g1, u0, u1, d0, d1, out):
    parts, chunks = 4, 7
    depth, width = D // parts, D // chunks
    blocks = NXY // parts
    acc = [jnp.zeros((128, 256), f32) for _ in range(2)]
    tot = jnp.zeros((1, 128), f32)
    for i in range(parts):
        k = slice(i * depth, (i + 1) * depth)
        group = slice(i * blocks, (i + 1) * blocks)
        wide = rows[group, : D // 16, :].reshape(depth, 128).T
        for j, (g, u) in enumerate(((g0, u0), (g1, u1))):
            acc[j] += jnp.dot(wide, jnp.concatenate([g[k, :], u[k, :]], axis=1), preferred_element_type=f32)
        tot += jnp.sum(rows[group, D // 16 :, :].astype(f32), axis=(0, 1))[None]
    inv = lax.rsqrt(tot / D + 1e-06).T
    scale = weight[...].T
    inner = []
    for j in range(2):
        gate = acc[j][:, :128] * inv
        up = acc[j][:, 128:] * inv
        inner.append((gate / (1.0 + jnp.exp(-gate)) * up * scale).astype(bf16))
    inner = jnp.concatenate(inner, axis=1)
    for n in range(chunks):
        c = slice(n * width, (n + 1) * width)
        down = jnp.concatenate([d0[:, c], d1[:, c]], axis=0)
        out[:, c] = jnp.dot(inner, down, preferred_element_type=f32).astype(bf16)


def experts(rows, weight, *weights):
    near = pl.BlockSpec(memory_space=pltpu.VMEM)
    return pl.pallas_call(
        experts_kernel,
        in_specs=[near] * 8,
        out_specs=near,
        out_shape=jax.ShapeDtypeStruct((128, D), bf16),
        compiler_params=pltpu.CompilerParams(vmem_limit_bytes=24 * 1024 * 1024),
        cost_estimate=pl.CostEstimate(flops=705_000_000, bytes_accessed=15_000_000, transcendentals=32768),
    )(rows, weight, *weights)


def body(
    query_latent,
    query_rope,
    cache_latent,
    cache_rope,
    new_latent,
    new_rope,
    cache_lengths,
    row_counts,
    value_up,
    out_proj,
    norm_gain,
    expert_ids,
    route_gates,
    gate_proj,
    up_proj,
    down_proj,
):
    core = lax.axis_index("c")
    column = lax.axis_index(XY)

    out_other = lax.ppermute(out_proj, "c", SWAP)
    gate_other = lax.ppermute(gate_proj, "c", SWAP)
    up_other = lax.ppermute(up_proj, "c", SWAP)
    down_other = lax.ppermute(down_proj, "c", SWAP)

    ctx = attend(
        lax.axis_index(DP)[None],
        cache_lengths,
        row_counts,
        query_latent,
        query_rope,
        cache_latent,
        cache_rope,
        new_latent,
        new_rope,
        value_up,
    )
    ctx = jnp.broadcast_to(ctx.reshape(1, STEPS, SLOTS, -1), (NH, STEPS, SLOTS, ctx.shape[1]))
    ctx = lax.all_to_all(ctx.reshape(NH * 2, SLOTS, -1), ("h", "c"), 0, 0).reshape(NH, 2, SLOTS, -1)
    ctx, expert_ids, route_gates, row_counts, norm_gain, out_other, gate_other, up_other, down_other = (
        lax.optimization_barrier(
            (ctx, expert_ids, route_gates, row_counts, norm_gain, out_other, gate_other, up_other, down_other)
        )
    )

    def prepare():
        gain = lax.dynamic_slice_in_dim(norm_gain, column * (D // 16), D // 16, 0)
        fours = jnp.sum(jnp.where(expert_ids == column, route_gates, 0.0), axis=2)
        live = (jnp.arange(SLOTS)[None, :] < row_counts[:, None]).astype(f32).reshape(1, 128)
        return jnp.broadcast_to(gain[:, None], (D // 16, 128)), fours * live

    def leave():
        return jnp.zeros((D // 16, 128), f32), jnp.zeros((STEPS, 128), f32)

    gain, weight = lax.cond(core == 0, prepare, leave)
    ctx, gain, weight = lax.optimization_barrier((ctx, gain, weight))
    gain = jnp.where(core == 0, gain, lax.ppermute(gain, "c", ((0, 1),)))
    weight = jnp.where(core == 0, weight, lax.ppermute(weight, "c", ((0, 1),)))
    weight = lax.dynamic_slice_in_dim(weight, core, 1, 0)

    ctx = jnp.where(core == 0, ctx, ctx[:, ::-1])
    ctx = jnp.transpose(ctx, (0, 2, 1, 3)).reshape(8, -1)
    ctx = spread(ctx, XY, NXY).reshape(128, -1)

    half = ctx.shape[1] // 2
    part = jnp.dot(ctx[:, :half], out_proj, preferred_element_type=f32)
    part = part + jnp.dot(ctx[:, half:], out_other, preferred_element_type=f32)
    chip = part.T.astype(bf16)
    pieces = spread(chip, Z, NZ).reshape(NH, 2, D // 64, 128).astype(f32)
    hid = jnp.sum(pieces, axis=1).astype(bf16)
    own_hid = lax.dynamic_index_in_dim(hid, lax.axis_index("h"), 0, keepdims=False)

    hid_f = hid.astype(f32).reshape(D // 16, 128)
    scaled = (hid_f * gain).astype(bf16)
    squares = jnp.sum(hid_f * hid_f, axis=0, keepdims=True)
    high = squares.astype(bf16)
    low = (squares - high.astype(f32)).astype(bf16)
    packed = jnp.concatenate([scaled, high, low, jnp.zeros((14, 128), bf16)], axis=0)
    packed, own_hid = lax.optimization_barrier((packed, own_hid))
    rows = spread(packed, XY, NXY)
    rows, own_hid = lax.optimization_barrier((rows, own_hid))

    out = experts(rows, weight, gate_proj, gate_other, up_proj, up_other, down_proj, down_other)
    out, own_hid = lax.optimization_barrier((out, own_hid))
    got = lax.all_to_all(out.reshape(NXY, 8, D), XY, 0, 0)
    got, own_hid = lax.optimization_barrier((got, own_hid))
    sums = jnp.sum(got.astype(f32), axis=0).astype(bf16)
    sums = jnp.transpose(sums.reshape(NH, SLOTS, 4, D // 4), (0, 2, 1, 3)).reshape(16, SLOTS, D // 4)

    other_hid = lax.ppermute(own_hid, "c", SWAP)
    steps = jnp.where(core == 0, jnp.stack([own_hid, other_hid]), jnp.stack([other_hid, own_hid]))
    hidden = jnp.transpose(steps, (0, 2, 1))

    own = lax.all_to_all(sums, ("h", "l", "c"), 0, 0)
    mixed = jnp.sum(own.astype(f32).reshape(NZ, STEPS, SLOTS, D // 4), axis=0).astype(bf16)
    return hidden, mixed


def solution(mesh):
    fine = Mesh(mesh.devices.reshape(4, 4, 4, 2, 2), ("x", "y", "h", "l", "c"))
    return jax.shard_map(
        body,
        mesh=fine,
        in_specs=(
            P(None, DP, TP),
            P(None, DP, TP),
            P(DP, None, None),
            P(DP, None, None),
            P(None, DP, None),
            P(None, DP, None),
            P(DP),
            P(),
            P(TP, None, None),
            P(TP, DP),
            P(),
            P(),
            P(),
            P(None, DP + TP),
            P(None, DP + TP),
            P(DP + TP, None),
        ),
        out_specs=(P(None, None, DP), P(None, DP, TP)),
        check_vma=False,
    )
```

```python
import jax
import jax.numpy as jnp
from jax import lax
from jax.experimental import pallas as pl
from jax.experimental.pallas import tpu as pltpu
from jax.sharding import Mesh, PartitionSpec as P

D = 7168
LAT = 512
ROPE = 64
HD = 128
FFN = 2048
STEPS = 2
SLOTS = 2
CACHE = 384

DP = ("x", "y", "h")
TP = ("l", "c")
XY = ("x", "y")
Z = ("h", "l")
NXY = 16
NZ = 8
NH = 4
SWAP = ((0, 1), (1, 0))

bf16 = jnp.bfloat16
f32 = jnp.float32


def spread(value, axes, count):
    copies = jnp.broadcast_to(value[None], (count,) + value.shape)
    return lax.all_to_all(copies, axes, 0, 0)


def attend_kernel(place, lengths, counts, ql_hbm, qr_hbm, cl_hbm, cr_hbm, nl_hbm, nr_hbm, v_hbm, out,
                  ql, qr, cl, cr, nl, nr, v, q_rows, r_rows, lat, sems):
    pairs = ((ql_hbm, ql), (qr_hbm, qr), (cl_hbm, cl), (cr_hbm, cr), (nl_hbm, nl), (nr_hbm, nr), (v_hbm, v))
    copies = [pltpu.make_async_copy(src, dst, sems.at[i]) for i, (src, dst) in enumerate(pairs)]
    for copy in copies:
        copy.start()
    heads = v.shape[0]
    rows = STEPS * heads
    scale = (HD + ROPE) ** (-0.5)
    copies[0].wait()
    copies[1].wait()
    for s in range(STEPS):
        for h in range(heads):
            q_rows[:, s * heads + h, :] = ql[s, :, h * LAT : (h + 1) * LAT].astype(f32)
        for p in range(heads // 2):
            pair = qr[s, :, p * 2 * ROPE : (p + 1) * 2 * ROPE].astype(f32)
            r_rows[:, s * heads + 2 * p, :] = pair
            r_rows[:, s * heads + 2 * p + 1, :] = pair
    for copy in copies[2:6]:
        copy.wait()
    step_of_row = lax.broadcasted_iota(jnp.int32, (rows, 1), 0) // heads
    position = lax.broadcasted_iota(jnp.int32, (rows, CACHE), 1)
    row_id = lax.broadcasted_iota(jnp.int32, (rows, 2 * ROPE), 0)
    lane_id = lax.broadcasted_iota(jnp.int32, (rows, 2 * ROPE), 1)
    own_half = row_id % 2 == lane_id // ROPE
    dims = (((1,), (1,)), ((), ()))
    for b in range(SLOTS):
        qf = q_rows[b]
        rf = jnp.where(own_half, r_rows[b], 0.0)
        rope = jnp.concatenate([cr[b], cr[b]], axis=0)
        old = lax.dot_general(qf.astype(bf16), cl[b], dims, preferred_element_type=f32)
        old = (old + jnp.dot(rf.astype(bf16), rope, preferred_element_type=f32)) * scale
        old = jnp.where(position < lengths[b], old, -1e30)
        top = jnp.max(old, axis=1, keepdims=True)
        new = []
        for i in range(STEPS):
            fresh_rope = nr[i, b : b + 1, :].astype(f32)
            n = jnp.sum(qf * nl[i, b : b + 1, :].astype(f32), axis=1, keepdims=True)
            n += jnp.sum(rf * jnp.concatenate([fresh_rope, fresh_rope], axis=1), axis=1, keepdims=True)
            n = jnp.where(step_of_row >= i, n * scale, -1e30)
            new.append(n)
            top = jnp.maximum(top, n)
        old = jnp.exp(old - top)
        new = [jnp.exp(n - top) for n in new]
        total = jnp.sum(old, axis=1, keepdims=True) + new[0] + new[1]
        res = jnp.dot((old / total).astype(bf16), cl[b], preferred_element_type=f32)
        for i in range(STEPS):
            res += (new[i] / total).astype(bf16).astype(f32) * nl[i, b : b + 1, :].astype(f32)
        for s in range(STEPS):
            lat[:, s * SLOTS + b, :] = res[s * heads : (s + 1) * heads, :]
    copies[6].wait()
    slot = lax.broadcasted_iota(jnp.int32, (STEPS * SLOTS, HD), 0) % SLOTS
    live = slot < counts[place[0]]
    for h in range(heads):
        ctx = jnp.dot(lat[h].astype(bf16), v[h], preferred_element_type=f32)
        out[:, h * HD : (h + 1) * HD] = jnp.where(live, ctx[: STEPS * SLOTS], 0.0).astype(bf16)


def attend(place, lengths, counts, *arrays):
    heads = arrays[-1].shape[0]
    scalars = pl.BlockSpec(memory_space=pltpu.SMEM)
    far = pl.BlockSpec(memory_space=pl.ANY)
    return pl.pallas_call(
        attend_kernel,
        in_specs=[scalars] * 3 + [far] * 7,
        out_specs=pl.BlockSpec(memory_space=pltpu.VMEM),
        out_shape=jax.ShapeDtypeStruct((STEPS * SLOTS, heads * HD), bf16),
        scratch_shapes=[pltpu.VMEM(a.shape, bf16) for a in arrays]
        + [
            pltpu.VMEM((SLOTS, STEPS * heads, LAT), f32),
            pltpu.VMEM((SLOTS, STEPS * heads, 2 * ROPE), f32),
            pltpu.VMEM((heads, 8, LAT), f32),
            pltpu.SemaphoreType.DMA((7,)),
        ],
        cost_estimate=pl.CostEstimate(flops=160_000_000, bytes_accessed=6_000_000, transcendentals=50_000),
    )(place, lengths, counts, *arrays)


def experts_kernel(rows, weight, g0, g1, u0, u1, d0, d1, out):
    parts, chunks = 4, 7
    depth, width = D // parts, D // chunks
    blocks = NXY // parts
    acc = [jnp.zeros((128, 256), f32) for _ in range(2)]
    tot = jnp.zeros((1, 128), f32)
    for i in range(parts):
        k = slice(i * depth, (i + 1) * depth)
        group = slice(i * blocks, (i + 1) * blocks)
        wide = rows[group, : D // 16, :].reshape(depth, 128).T
        for j, (g, u) in enumerate(((g0, u0), (g1, u1))):
            acc[j] += jnp.dot(wide, jnp.concatenate([g[k, :], u[k, :]], axis=1), preferred_element_type=f32)
        tot += jnp.sum(rows[group, D // 16 :, :].astype(f32), axis=(0, 1))[None]
    inv = lax.rsqrt(tot / D + 1e-06).T
    scale = weight[...].T
    inner = []
    for j in range(2):
        gate = acc[j][:, :128] * inv
        up = acc[j][:, 128:] * inv
        inner.append((gate / (1.0 + jnp.exp(-gate)) * up * scale).astype(bf16))
    inner = jnp.concatenate(inner, axis=1)
    for n in range(chunks):
        c = slice(n * width, (n + 1) * width)
        down = jnp.concatenate([d0[:, c], d1[:, c]], axis=0)
        out[:, c] = jnp.dot(inner, down, preferred_element_type=f32).astype(bf16)


def experts(rows, weight, *weights):
    near = pl.BlockSpec(memory_space=pltpu.VMEM)
    return pl.pallas_call(
        experts_kernel,
        in_specs=[near] * 8,
        out_specs=near,
        out_shape=jax.ShapeDtypeStruct((128, D), bf16),
        compiler_params=pltpu.CompilerParams(vmem_limit_bytes=24 * 1024 * 1024),
        cost_estimate=pl.CostEstimate(flops=705_000_000, bytes_accessed=15_000_000, transcendentals=32768),
    )(rows, weight, *weights)


def body(
    query_latent,
    query_rope,
    cache_latent,
    cache_rope,
    new_latent,
    new_rope,
    cache_lengths,
    row_counts,
    value_up,
    out_proj,
    norm_gain,
    expert_ids,
    route_gates,
    gate_proj,
    up_proj,
    down_proj,
):
    core = lax.axis_index("c")
    column = lax.axis_index(XY)

    out_other = lax.ppermute(out_proj, "c", SWAP)
    gate_other = lax.ppermute(gate_proj, "c", SWAP)
    up_other = lax.ppermute(up_proj, "c", SWAP)
    down_other = lax.ppermute(down_proj, "c", SWAP)

    ctx = attend(
        lax.axis_index(DP)[None],
        cache_lengths,
        row_counts,
        query_latent,
        query_rope,
        cache_latent,
        cache_rope,
        new_latent,
        new_rope,
        value_up,
    )
    ctx = jnp.broadcast_to(ctx.reshape(1, STEPS, SLOTS, -1), (NH, STEPS, SLOTS, ctx.shape[1]))
    ctx = lax.all_to_all(ctx.reshape(NH * 2, SLOTS, -1), ("h", "c"), 0, 0).reshape(NH, 2, SLOTS, -1)
    gain = lax.dynamic_slice_in_dim(norm_gain, column * (D // 16), D // 16, 0)
    gain = jnp.broadcast_to(gain[:, None], (D // 16, 128))
    fours = jnp.sum(jnp.where(expert_ids == column, route_gates, 0.0), axis=2)
    live = (jnp.arange(SLOTS)[None, :] < row_counts[:, None]).astype(f32).reshape(1, 128)
    weight = lax.dynamic_slice_in_dim(fours, core, 1, 0) * live
    ctx, gain, weight, out_other, gate_other, up_other, down_other = lax.optimization_barrier(
        (ctx, gain, weight, out_other, gate_other, up_other, down_other)
    )
    ctx = jnp.where(core == 0, ctx, ctx[:, ::-1])
    ctx = jnp.transpose(ctx, (0, 2, 1, 3)).reshape(8, -1)
    ctx = spread(ctx, XY, NXY).reshape(128, -1)

    half = ctx.shape[1] // 2
    part = jnp.dot(ctx[:, :half], out_proj, preferred_element_type=f32)
    part = part + jnp.dot(ctx[:, half:], out_other, preferred_element_type=f32)
    chip = part.T.astype(bf16)
    pieces = spread(chip, Z, NZ).reshape(NH, 2, D // 64, 128).astype(f32)
    hid = jnp.sum(pieces, axis=1).astype(bf16)
    own_hid = lax.dynamic_index_in_dim(hid, lax.axis_index("h"), 0, keepdims=False)

    hid_f = hid.astype(f32).reshape(D // 16, 128)
    scaled = (hid_f * gain).astype(bf16)
    squares = jnp.sum(hid_f * hid_f, axis=0, keepdims=True)
    high = squares.astype(bf16)
    low = (squares - high.astype(f32)).astype(bf16)
    packed = jnp.concatenate([scaled, high, low, jnp.zeros((14, 128), bf16)], axis=0)
    packed, own_hid = lax.optimization_barrier((packed, own_hid))
    rows = spread(packed, XY, NXY)
    rows, own_hid = lax.optimization_barrier((rows, own_hid))

    out = experts(rows, weight, gate_proj, gate_other, up_proj, up_other, down_proj, down_other)
    out, own_hid = lax.optimization_barrier((out, own_hid))
    got = lax.all_to_all(out.reshape(NXY, 8, D), XY, 0, 0)
    got, own_hid = lax.optimization_barrier((got, own_hid))
    sums = jnp.sum(got.astype(f32), axis=0).astype(bf16)
    sums = jnp.transpose(sums.reshape(NH, SLOTS, 4, D // 4), (0, 2, 1, 3)).reshape(16, SLOTS, D // 4)

    other_hid = lax.ppermute(own_hid, "c", SWAP)
    steps = jnp.where(core == 0, jnp.stack([own_hid, other_hid]), jnp.stack([other_hid, own_hid]))
    hidden = jnp.transpose(steps, (0, 2, 1))

    own = lax.all_to_all(sums, ("h", "l", "c"), 0, 0)
    mixed = jnp.sum(own.astype(f32).reshape(NZ, STEPS, SLOTS, D // 4), axis=0).astype(bf16)
    return hidden, mixed


def solution(mesh):
    fine = Mesh(mesh.devices.reshape(4, 4, 4, 2, 2), ("x", "y", "h", "l", "c"))
    return jax.shard_map(
        body,
        mesh=fine,
        in_specs=(
            P(None, DP, TP),
            P(None, DP, TP),
            P(DP, None, None),
            P(DP, None, None),
            P(None, DP, None),
            P(None, DP, None),
            P(DP),
            P(),
            P(TP, None, None),
            P(TP, DP),
            P(),
            P(),
            P(),
            P(None, DP + TP),
            P(None, DP + TP),
            P(DP + TP, None),
        ),
        out_specs=(P(None, None, DP), P(None, DP, TP)),
        check_vma=False,
    )
```

```python
import jax
import jax.numpy as jnp
from jax import lax
from jax.experimental import pallas as pl
from jax.experimental.pallas import tpu as pltpu
from jax.sharding import Mesh, PartitionSpec as P

D = 7168
LAT = 512
ROPE = 64
HD = 128
FFN = 2048
STEPS = 2
SLOTS = 2
CACHE = 384

DP = ("x", "y", "h")
TP = ("l", "c")
XY = ("x", "y")
Z = ("h", "l")
NXY = 16
NZ = 8
NH = 4
SWAP = ((0, 1), (1, 0))

bf16 = jnp.bfloat16
f32 = jnp.float32


def spread(value, axes, count):
    copies = jnp.broadcast_to(value[None], (count,) + value.shape)
    return lax.all_to_all(copies, axes, 0, 0)


def attend_kernel(place, lengths, counts, ql_hbm, qr_hbm, cl_hbm, cr_hbm, nl_hbm, nr_hbm, v_hbm, out,
                  ql, qr, cl, cr, nl, nr, v, q_rows, r_rows, lat, sems):
    pairs = ((ql_hbm, ql), (qr_hbm, qr), (cl_hbm, cl), (cr_hbm, cr), (nl_hbm, nl), (nr_hbm, nr), (v_hbm, v))
    copies = [pltpu.make_async_copy(src, dst, sems.at[i]) for i, (src, dst) in enumerate(pairs)]
    for copy in copies:
        copy.start()
    heads = v.shape[0]
    rows = STEPS * heads
    scale = (HD + ROPE) ** (-0.5)
    copies[0].wait()
    copies[1].wait()
    for s in range(STEPS):
        for h in range(heads):
            q_rows[:, s * heads + h, :] = ql[s, :, h * LAT : (h + 1) * LAT].astype(f32)
        for p in range(heads // 2):
            pair = qr[s, :, p * 2 * ROPE : (p + 1) * 2 * ROPE].astype(f32)
            r_rows[:, s * heads + 2 * p, :] = pair
            r_rows[:, s * heads + 2 * p + 1, :] = pair
    for copy in copies[2:6]:
        copy.wait()
    step_of_row = lax.broadcasted_iota(jnp.int32, (rows, 1), 0) // heads
    position = lax.broadcasted_iota(jnp.int32, (rows, CACHE), 1)
    row_id = lax.broadcasted_iota(jnp.int32, (rows, 2 * ROPE), 0)
    lane_id = lax.broadcasted_iota(jnp.int32, (rows, 2 * ROPE), 1)
    own_half = row_id % 2 == lane_id // ROPE
    dims = (((1,), (1,)), ((), ()))
    for b in range(SLOTS):
        qf = q_rows[b]
        rf = jnp.where(own_half, r_rows[b], 0.0)
        rope = jnp.concatenate([cr[b], cr[b]], axis=0)
        old = lax.dot_general(qf.astype(bf16), cl[b], dims, preferred_element_type=f32)
        old = (old + jnp.dot(rf.astype(bf16), rope, preferred_element_type=f32)) * scale
        old = jnp.where(position < lengths[b], old, -1e30)
        top = jnp.max(old, axis=1, keepdims=True)
        new = []
        for i in range(STEPS):
            fresh_rope = nr[i, b : b + 1, :].astype(f32)
            n = jnp.sum(qf * nl[i, b : b + 1, :].astype(f32), axis=1, keepdims=True)
            n += jnp.sum(rf * jnp.concatenate([fresh_rope, fresh_rope], axis=1), axis=1, keepdims=True)
            n = jnp.where(step_of_row >= i, n * scale, -1e30)
            new.append(n)
            top = jnp.maximum(top, n)
        old = jnp.exp(old - top)
        new = [jnp.exp(n - top) for n in new]
        total = jnp.sum(old, axis=1, keepdims=True) + new[0] + new[1]
        res = jnp.dot((old / total).astype(bf16), cl[b], preferred_element_type=f32)
        for i in range(STEPS):
            res += (new[i] / total).astype(bf16).astype(f32) * nl[i, b : b + 1, :].astype(f32)
        for s in range(STEPS):
            lat[:, s * SLOTS + b, :] = res[s * heads : (s + 1) * heads, :]
    copies[6].wait()
    slot = lax.broadcasted_iota(jnp.int32, (STEPS * SLOTS, HD), 0) % SLOTS
    live = slot < counts[place[0]]
    for h in range(heads):
        ctx = jnp.dot(lat[h].astype(bf16), v[h], preferred_element_type=f32)
        ctx = jnp.where(live, ctx[: STEPS * SLOTS], 0.0).astype(bf16)
        for to in range(NH):
            for s in range(STEPS):
                out[to * 2 + s, :, h * HD : (h + 1) * HD] = ctx[s * SLOTS : (s + 1) * SLOTS]


def attend(place, lengths, counts, *arrays):
    heads = arrays[-1].shape[0]
    scalars = pl.BlockSpec(memory_space=pltpu.SMEM)
    far = pl.BlockSpec(memory_space=pl.ANY)
    return pl.pallas_call(
        attend_kernel,
        in_specs=[scalars] * 3 + [far] * 7,
        out_specs=pl.BlockSpec(memory_space=pltpu.VMEM),
        out_shape=jax.ShapeDtypeStruct((NH * 2, SLOTS, heads * HD), bf16),
        scratch_shapes=[pltpu.VMEM(a.shape, bf16) for a in arrays]
        + [
            pltpu.VMEM((SLOTS, STEPS * heads, LAT), f32),
            pltpu.VMEM((SLOTS, STEPS * heads, 2 * ROPE), f32),
            pltpu.VMEM((heads, 8, LAT), f32),
            pltpu.SemaphoreType.DMA((7,)),
        ],
        cost_estimate=pl.CostEstimate(flops=160_000_000, bytes_accessed=6_000_000, transcendentals=50_000),
    )(place, lengths, counts, *arrays)


def experts_kernel(rows, weight, g0, g1, u0, u1, d0, d1, out):
    parts, chunks = 4, 7
    depth, width = D // parts, D // chunks
    blocks = NXY // parts
    acc = [jnp.zeros((128, 256), f32) for _ in range(2)]
    tot = jnp.zeros((1, 128), f32)
    for i in range(parts):
        k = slice(i * depth, (i + 1) * depth)
        group = slice(i * blocks, (i + 1) * blocks)
        wide = rows[group, : D // 16, :].reshape(depth, 128).T
        for j, (g, u) in enumerate(((g0, u0), (g1, u1))):
            acc[j] += jnp.dot(wide, jnp.concatenate([g[k, :], u[k, :]], axis=1), preferred_element_type=f32)
        tot += jnp.sum(rows[group, D // 16 :, :].astype(f32), axis=(0, 1))[None]
    inv = lax.rsqrt(tot / D + 1e-06).T
    scale = weight[...].T
    inner = []
    for j in range(2):
        gate = acc[j][:, :128] * inv
        up = acc[j][:, 128:] * inv
        inner.append((gate / (1.0 + jnp.exp(-gate)) * up * scale).astype(bf16))
    inner = jnp.concatenate(inner, axis=1)
    for n in range(chunks):
        c = slice(n * width, (n + 1) * width)
        down = jnp.concatenate([d0[:, c], d1[:, c]], axis=0)
        out[:, c] = jnp.dot(inner, down, preferred_element_type=f32).astype(bf16)


def experts(rows, weight, *weights):
    near = pl.BlockSpec(memory_space=pltpu.VMEM)
    return pl.pallas_call(
        experts_kernel,
        in_specs=[near] * 8,
        out_specs=near,
        out_shape=jax.ShapeDtypeStruct((128, D), bf16),
        compiler_params=pltpu.CompilerParams(vmem_limit_bytes=24 * 1024 * 1024),
        cost_estimate=pl.CostEstimate(flops=705_000_000, bytes_accessed=15_000_000, transcendentals=32768),
    )(rows, weight, *weights)


def body(
    query_latent,
    query_rope,
    cache_latent,
    cache_rope,
    new_latent,
    new_rope,
    cache_lengths,
    row_counts,
    value_up,
    out_proj,
    norm_gain,
    expert_ids,
    route_gates,
    gate_proj,
    up_proj,
    down_proj,
):
    core = lax.axis_index("c")
    column = lax.axis_index(XY)

    out_other = lax.ppermute(out_proj, "c", SWAP)
    gate_other = lax.ppermute(gate_proj, "c", SWAP)
    up_other = lax.ppermute(up_proj, "c", SWAP)
    down_other = lax.ppermute(down_proj, "c", SWAP)

    ctx = attend(
        lax.axis_index(DP)[None],
        cache_lengths,
        row_counts,
        query_latent,
        query_rope,
        cache_latent,
        cache_rope,
        new_latent,
        new_rope,
        value_up,
    )
    ctx = lax.all_to_all(ctx, ("h", "c"), 0, 0).reshape(NH, 2, SLOTS, -1)
    gain = lax.dynamic_slice_in_dim(norm_gain, column * (D // 16), D // 16, 0)
    gain = jnp.broadcast_to(gain[:, None], (D // 16, 128))
    fours = jnp.sum(jnp.where(expert_ids == column, route_gates, 0.0), axis=2)
    live = (jnp.arange(SLOTS)[None, :] < row_counts[:, None]).astype(f32).reshape(1, 128)
    weight = lax.dynamic_slice_in_dim(fours, core, 1, 0) * live
    ctx, gain, weight, out_other, gate_other, up_other, down_other = lax.optimization_barrier(
        (ctx, gain, weight, out_other, gate_other, up_other, down_other)
    )
    ctx = lax.cond(core == 0, lambda v: jnp.stack([v[:, 1], v[:, 0]], axis=1), lambda v: v, ctx)
    ctx = jnp.transpose(ctx, (0, 2, 1, 3)).reshape(8, -1)
    ctx = spread(ctx, XY, NXY).reshape(128, -1)

    half = ctx.shape[1] // 2
    part = jnp.dot(ctx[:, :half], out_other, preferred_element_type=f32)
    part = part + jnp.dot(ctx[:, half:], out_proj, preferred_element_type=f32)
    chip = part.T.astype(bf16)
    pieces = spread(chip, Z, NZ).reshape(NH, 2, D // 64, 128).astype(f32)
    hid = jnp.sum(pieces, axis=1).astype(bf16)
    own_hid = lax.dynamic_index_in_dim(hid, lax.axis_index("h"), 0, keepdims=False)

    hid_f = hid.astype(f32).reshape(D // 16, 128)
    scaled = (hid_f * gain).astype(bf16)
    squares = jnp.sum(hid_f * hid_f, axis=0, keepdims=True)
    high = squares.astype(bf16)
    low = (squares - high.astype(f32)).astype(bf16)
    packed = jnp.concatenate([scaled, high, low, jnp.zeros((14, 128), bf16)], axis=0)
    packed, own_hid = lax.optimization_barrier((packed, own_hid))
    rows = spread(packed, XY, NXY)
    rows, own_hid = lax.optimization_barrier((rows, own_hid))

    out = experts(rows, weight, gate_proj, gate_other, up_proj, up_other, down_proj, down_other)
    out, own_hid = lax.optimization_barrier((out, own_hid))
    got = lax.all_to_all(out.reshape(NXY, 8, D), XY, 0, 0)
    got, own_hid = lax.optimization_barrier((got, own_hid))
    sums = jnp.sum(got.astype(f32), axis=0).astype(bf16)
    sums = jnp.transpose(sums.reshape(NH, SLOTS, 4, D // 4), (0, 2, 1, 3)).reshape(16, SLOTS, D // 4)

    other_hid = lax.ppermute(own_hid, "c", SWAP)
    steps = jnp.where(core == 0, jnp.stack([own_hid, other_hid]), jnp.stack([other_hid, own_hid]))
    hidden = jnp.transpose(steps, (0, 2, 1))

    own = lax.all_to_all(sums, ("h", "l", "c"), 0, 0)
    mixed = jnp.sum(own.astype(f32).reshape(NZ, STEPS, SLOTS, D // 4), axis=0).astype(bf16)
    return hidden, mixed


def solution(mesh):
    fine = Mesh(mesh.devices.reshape(4, 4, 4, 2, 2), ("x", "y", "h", "l", "c"))
    return jax.shard_map(
        body,
        mesh=fine,
        in_specs=(
            P(None, DP, TP),
            P(None, DP, TP),
            P(DP, None, None),
            P(DP, None, None),
            P(None, DP, None),
            P(None, DP, None),
            P(DP),
            P(),
            P(TP, None, None),
            P(TP, DP),
            P(),
            P(),
            P(),
            P(None, DP + TP),
            P(None, DP + TP),
            P(DP + TP, None),
        ),
        out_specs=(P(None, None, DP), P(None, DP, TP)),
        check_vma=False,
    )
```

```python
import jax
import jax.numpy as jnp
from jax import lax
from jax.experimental import pallas as pl
from jax.experimental.pallas import tpu as pltpu
from jax.sharding import Mesh, PartitionSpec as P

D = 7168
LAT = 512
ROPE = 64
HD = 128
FFN = 2048
STEPS = 2
SLOTS = 2
CACHE = 384

DP = ("x", "y", "h")
TP = ("l", "c")
XY = ("x", "y")
Z = ("h", "l")
NXY = 16
NZ = 8
NH = 4
SWAP = ((0, 1), (1, 0))

bf16 = jnp.bfloat16
f32 = jnp.float32


def spread(value, axes, count):
    copies = jnp.broadcast_to(value[None], (count,) + value.shape)
    return lax.all_to_all(copies, axes, 0, 0)


def attend_kernel(place, lengths, counts, ql_hbm, qr_hbm, cl_hbm, cr_hbm, nl_hbm, nr_hbm, v_hbm, out,
                  ql, qr, cl, cr, nl, nr, v, q_rows, r_rows, lat, sems):
    pairs = ((ql_hbm, ql), (qr_hbm, qr), (cl_hbm, cl), (cr_hbm, cr), (nl_hbm, nl), (nr_hbm, nr), (v_hbm, v))
    copies = [pltpu.make_async_copy(src, dst, sems.at[i]) for i, (src, dst) in enumerate(pairs)]
    for copy in copies:
        copy.start()
    heads = v.shape[0]
    rows = STEPS * heads
    scale = (HD + ROPE) ** (-0.5)
    copies[0].wait()
    copies[1].wait()
    for s in range(STEPS):
        for h in range(heads):
            q_rows[:, s * heads + h, :] = ql[s, :, h * LAT : (h + 1) * LAT].astype(f32)
        for p in range(heads // 2):
            pair = qr[s, :, p * 2 * ROPE : (p + 1) * 2 * ROPE].astype(f32)
            r_rows[:, s * heads + 2 * p, :] = pair
            r_rows[:, s * heads + 2 * p + 1, :] = pair
    for copy in copies[2:6]:
        copy.wait()
    step_of_row = lax.broadcasted_iota(jnp.int32, (rows, 1), 0) // heads
    position = lax.broadcasted_iota(jnp.int32, (rows, CACHE), 1)
    row_id = lax.broadcasted_iota(jnp.int32, (rows, 2 * ROPE), 0)
    lane_id = lax.broadcasted_iota(jnp.int32, (rows, 2 * ROPE), 1)
    own_half = row_id % 2 == lane_id // ROPE
    dims = (((1,), (1,)), ((), ()))
    for b in range(SLOTS):
        qf = q_rows[b]
        rf = jnp.where(own_half, r_rows[b], 0.0)
        rope = jnp.concatenate([cr[b], cr[b]], axis=0)
        old = lax.dot_general(qf.astype(bf16), cl[b], dims, preferred_element_type=f32)
        old = (old + jnp.dot(rf.astype(bf16), rope, preferred_element_type=f32)) * scale
        old = jnp.where(position < lengths[b], old, -1e30)
        top = jnp.max(old, axis=1, keepdims=True)
        new = []
        for i in range(STEPS):
            fresh_rope = nr[i, b : b + 1, :].astype(f32)
            n = jnp.sum(qf * nl[i, b : b + 1, :].astype(f32), axis=1, keepdims=True)
            n += jnp.sum(rf * jnp.concatenate([fresh_rope, fresh_rope], axis=1), axis=1, keepdims=True)
            n = jnp.where(step_of_row >= i, n * scale, -1e30)
            new.append(n)
            top = jnp.maximum(top, n)
        old = jnp.exp(old - top)
        new = [jnp.exp(n - top) for n in new]
        total = jnp.sum(old, axis=1, keepdims=True) + new[0] + new[1]
        res = jnp.dot((old / total).astype(bf16), cl[b], preferred_element_type=f32)
        for i in range(STEPS):
            res += (new[i] / total).astype(bf16).astype(f32) * nl[i, b : b + 1, :].astype(f32)
        for s in range(STEPS):
            lat[:, s * SLOTS + b, :] = res[s * heads : (s + 1) * heads, :]
    copies[6].wait()
    slot = lax.broadcasted_iota(jnp.int32, (STEPS * SLOTS, HD), 0) % SLOTS
    live = slot < counts[place[0]]
    for h in range(heads):
        ctx = jnp.dot(lat[h].astype(bf16), v[h], preferred_element_type=f32)
        ctx = jnp.where(live, ctx[: STEPS * SLOTS], 0.0).astype(bf16)
        for to in range(NH):
            for s in range(STEPS):
                out[to * 2 + s, :, h * HD : (h + 1) * HD] = ctx[s * SLOTS : (s + 1) * SLOTS]


def attend(place, lengths, counts, *arrays):
    heads = arrays[-1].shape[0]
    scalars = pl.BlockSpec(memory_space=pltpu.SMEM)
    far = pl.BlockSpec(memory_space=pl.ANY)
    return pl.pallas_call(
        attend_kernel,
        in_specs=[scalars] * 3 + [far] * 7,
        out_specs=pl.BlockSpec(memory_space=pltpu.VMEM),
        out_shape=jax.ShapeDtypeStruct((NH * 2, SLOTS, heads * HD), bf16),
        scratch_shapes=[pltpu.VMEM(a.shape, bf16) for a in arrays]
        + [
            pltpu.VMEM((SLOTS, STEPS * heads, LAT), f32),
            pltpu.VMEM((SLOTS, STEPS * heads, 2 * ROPE), f32),
            pltpu.VMEM((heads, 8, LAT), f32),
            pltpu.SemaphoreType.DMA((7,)),
        ],
        cost_estimate=pl.CostEstimate(flops=160_000_000, bytes_accessed=6_000_000, transcendentals=50_000),
    )(place, lengths, counts, *arrays)


def experts_kernel(rows, weight, g0, g1, u0, u1, d0, d1, out):
    parts, chunks = 4, 7
    depth, width = D // parts, D // chunks
    blocks = NXY // parts
    acc = [jnp.zeros((128, 256), f32) for _ in range(2)]
    tot = jnp.zeros((1, 128), f32)
    for i in range(parts):
        k = slice(i * depth, (i + 1) * depth)
        group = slice(i * blocks, (i + 1) * blocks)
        wide = rows[group, : D // 16, :].reshape(depth, 128).T
        for j, (g, u) in enumerate(((g0, u0), (g1, u1))):
            acc[j] += jnp.dot(wide, jnp.concatenate([g[k, :], u[k, :]], axis=1), preferred_element_type=f32)
        tot += jnp.sum(rows[group, D // 16 :, :].astype(f32), axis=(0, 1))[None]
    inv = lax.rsqrt(tot / D + 1e-06).T
    scale = weight[...].T
    inner = []
    for j in range(2):
        gate = acc[j][:, :128] * inv
        up = acc[j][:, 128:] * inv
        inner.append((gate / (1.0 + jnp.exp(-gate)) * up * scale).astype(bf16))
    inner = jnp.concatenate(inner, axis=1)
    for n in range(chunks):
        c = slice(n * width, (n + 1) * width)
        down = jnp.concatenate([d0[:, c], d1[:, c]], axis=0)
        out[:, c] = jnp.dot(inner, down, preferred_element_type=f32).astype(bf16)


def experts(rows, weight, *weights):
    near = pl.BlockSpec(memory_space=pltpu.VMEM)
    return pl.pallas_call(
        experts_kernel,
        in_specs=[near] * 8,
        out_specs=near,
        out_shape=jax.ShapeDtypeStruct((128, D), bf16),
        compiler_params=pltpu.CompilerParams(vmem_limit_bytes=24 * 1024 * 1024),
        cost_estimate=pl.CostEstimate(flops=705_000_000, bytes_accessed=15_000_000, transcendentals=32768),
    )(rows, weight, *weights)


def stage_kernel(a, b, to_a, to_b, sems):
    copies = [pltpu.make_async_copy(a, to_a, sems.at[0]), pltpu.make_async_copy(b, to_b, sems.at[1])]
    for copy in copies:
        copy.start()
    for copy in copies:
        copy.wait()


def stage(*arrays):
    return pl.pallas_call(
        stage_kernel,
        in_specs=[pl.BlockSpec(memory_space=pl.ANY)] * 2,
        out_specs=[pl.BlockSpec(memory_space=pltpu.VMEM)] * 2,
        out_shape=[jax.ShapeDtypeStruct(a.shape, a.dtype) for a in arrays],
        scratch_shapes=[pltpu.SemaphoreType.DMA((2,))],
    )(*arrays)


def unwritten(*arrays):
    return pl.pallas_call(
        lambda *outs: None,
        out_specs=[pl.BlockSpec(memory_space=pltpu.VMEM)] * 2,
        out_shape=[jax.ShapeDtypeStruct(a.shape, a.dtype) for a in arrays],
    )()


def body(
    query_latent,
    query_rope,
    cache_latent,
    cache_rope,
    new_latent,
    new_rope,
    cache_lengths,
    row_counts,
    value_up,
    out_proj,
    norm_gain,
    expert_ids,
    route_gates,
    gate_proj,
    up_proj,
    down_proj,
):
    core = lax.axis_index("c")
    column = lax.axis_index(XY)

    out_other = lax.ppermute(out_proj, "c", SWAP)
    gate_other = lax.ppermute(gate_proj, "c", SWAP)
    up_other = lax.ppermute(up_proj, "c", SWAP)
    down_other = lax.ppermute(down_proj, "c", SWAP)

    ctx = attend(
        lax.axis_index(DP)[None],
        cache_lengths,
        row_counts,
        query_latent,
        query_rope,
        cache_latent,
        cache_rope,
        new_latent,
        new_rope,
        value_up,
    )
    ctx = lax.all_to_all(ctx, ("h", "c"), 0, 0).reshape(NH, 2, SLOTS, -1)
    sources = (norm_gain, expert_ids, route_gates, row_counts, gate_proj, up_proj)
    blank = jnp.zeros((D // 16, 128), f32), jnp.zeros((1, 128), f32), *unwritten(gate_proj, up_proj)
    ctx, blank, sources, out_other, gate_other, up_other, down_other = lax.optimization_barrier(
        (ctx, blank, sources, out_other, gate_other, up_other, down_other)
    )

    def prepare(norm_gain, expert_ids, route_gates, row_counts, *weights):
        gain = lax.dynamic_slice_in_dim(norm_gain, column * (D // 16), D // 16, 0)
        fours = jnp.sum(jnp.where(expert_ids == column, route_gates, 0.0), axis=2)
        live = (jnp.arange(SLOTS)[None, :] < row_counts[:, None]).astype(f32).reshape(1, 128)
        return (
            jnp.broadcast_to(gain[:, None], (D // 16, 128)),
            lax.dynamic_slice_in_dim(fours, core, 1, 0) * live,
            *stage(*weights),
        )

    early = lax.cond(core == 0, lambda _, sources: prepare(*sources), lambda blank, _: blank, blank, sources)
    ctx, early = lax.optimization_barrier((ctx, early))
    ctx = lax.cond(core == 0, lambda v: jnp.stack([v[:, 1], v[:, 0]], axis=1), lambda v: v, ctx)
    ctx = jnp.transpose(ctx, (0, 2, 1, 3)).reshape(8, -1)
    ctx = spread(ctx, XY, NXY).reshape(128, -1)
    ctx, early, sources = lax.optimization_barrier((ctx, early, sources))
    gain, weight, gate_own, up_own = lax.cond(core == 0, lambda early, _: early, lambda _, sources: prepare(*sources), early, sources)

    half = ctx.shape[1] // 2
    part = jnp.dot(ctx[:, :half], out_other, preferred_element_type=f32)
    part = part + jnp.dot(ctx[:, half:], out_proj, preferred_element_type=f32)
    chip = part.T.astype(bf16)
    pieces = spread(chip, Z, NZ).reshape(NH, 2, D // 64, 128).astype(f32)
    hid = jnp.sum(pieces, axis=1).astype(bf16)
    own_hid = lax.dynamic_index_in_dim(hid, lax.axis_index("h"), 0, keepdims=False)

    hid_f = hid.astype(f32).reshape(D // 16, 128)
    scaled = (hid_f * gain).astype(bf16)
    squares = jnp.sum(hid_f * hid_f, axis=0, keepdims=True)
    high = squares.astype(bf16)
    low = (squares - high.astype(f32)).astype(bf16)
    packed = jnp.concatenate([scaled, high, low, jnp.zeros((14, 128), bf16)], axis=0)
    packed, own_hid = lax.optimization_barrier((packed, own_hid))
    rows = spread(packed, XY, NXY)
    rows, own_hid = lax.optimization_barrier((rows, own_hid))

    out = experts(rows, weight, gate_own, gate_other, up_own, up_other, down_proj, down_other)
    out, own_hid = lax.optimization_barrier((out, own_hid))
    got = lax.all_to_all(out.reshape(NXY, 8, D), XY, 0, 0)
    got, own_hid = lax.optimization_barrier((got, own_hid))
    sums = jnp.sum(got.astype(f32), axis=0).astype(bf16)
    sums = jnp.transpose(sums.reshape(NH, SLOTS, 4, D // 4), (0, 2, 1, 3)).reshape(16, SLOTS, D // 4)

    other_hid = lax.ppermute(own_hid, "c", SWAP)
    steps = jnp.where(core == 0, jnp.stack([own_hid, other_hid]), jnp.stack([other_hid, own_hid]))
    hidden = jnp.transpose(steps, (0, 2, 1))

    own = lax.all_to_all(sums, ("h", "l", "c"), 0, 0)
    mixed = jnp.sum(own.astype(f32).reshape(NZ, STEPS, SLOTS, D // 4), axis=0).astype(bf16)
    return hidden, mixed


def solution(mesh):
    fine = Mesh(mesh.devices.reshape(4, 4, 4, 2, 2), ("x", "y", "h", "l", "c"))
    return jax.shard_map(
        body,
        mesh=fine,
        in_specs=(
            P(None, DP, TP),
            P(None, DP, TP),
            P(DP, None, None),
            P(DP, None, None),
            P(None, DP, None),
            P(None, DP, None),
            P(DP),
            P(),
            P(TP, None, None),
            P(TP, DP),
            P(),
            P(),
            P(),
            P(None, DP + TP),
            P(None, DP + TP),
            P(DP + TP, None),
        ),
        out_specs=(P(None, None, DP), P(None, DP, TP)),
        check_vma=False,
    )
```

```python
import jax
import jax.numpy as jnp
from jax import lax
from jax.experimental import pallas as pl
from jax.experimental.pallas import tpu as pltpu
from jax.sharding import Mesh, PartitionSpec as P

D = 7168
LAT = 512
ROPE = 64
HD = 128
FFN = 2048
STEPS = 2
SLOTS = 2
CACHE = 384

DP = ("x", "y", "h")
TP = ("l", "c")
XY = ("x", "y")
Z = ("h", "l")
NXY = 16
NZ = 8
NH = 4
SWAP = ((0, 1), (1, 0))

bf16 = jnp.bfloat16
f32 = jnp.float32


def spread(value, axes, count):
    copies = jnp.broadcast_to(value[None], (count,) + value.shape)
    return lax.all_to_all(copies, axes, 0, 0)


def attend_kernel(place, lengths, counts, ql_hbm, qr_hbm, cl_hbm, cr_hbm, nl_hbm, nr_hbm, v_hbm, out,
                  ql, qr, cl, cr, nl, nr, v, q_rows, r_rows, lat, sems):
    pairs = ((ql_hbm, ql), (qr_hbm, qr), (cl_hbm, cl), (cr_hbm, cr), (nl_hbm, nl), (nr_hbm, nr), (v_hbm, v))
    copies = [pltpu.make_async_copy(src, dst, sems.at[i]) for i, (src, dst) in enumerate(pairs)]
    for copy in copies:
        copy.start()
    heads = v.shape[0]
    rows = STEPS * heads
    scale = (HD + ROPE) ** (-0.5)
    copies[0].wait()
    copies[1].wait()
    for s in range(STEPS):
        for h in range(heads):
            q_rows[:, s * heads + h, :] = ql[s, :, h * LAT : (h + 1) * LAT].astype(f32)
        for p in range(heads // 2):
            pair = qr[s, :, p * 2 * ROPE : (p + 1) * 2 * ROPE].astype(f32)
            r_rows[:, s * heads + 2 * p, :] = pair
            r_rows[:, s * heads + 2 * p + 1, :] = pair
    for copy in copies[2:6]:
        copy.wait()
    step_of_row = lax.broadcasted_iota(jnp.int32, (rows, 1), 0) // heads
    position = lax.broadcasted_iota(jnp.int32, (rows, CACHE), 1)
    row_id = lax.broadcasted_iota(jnp.int32, (rows, 2 * ROPE), 0)
    lane_id = lax.broadcasted_iota(jnp.int32, (rows, 2 * ROPE), 1)
    own_half = row_id % 2 == lane_id // ROPE
    dims = (((1,), (1,)), ((), ()))
    for b in range(SLOTS):
        qf = q_rows[b]
        rf = jnp.where(own_half, r_rows[b], 0.0)
        rope = jnp.concatenate([cr[b], cr[b]], axis=0)
        old = lax.dot_general(qf.astype(bf16), cl[b], dims, preferred_element_type=f32)
        old = (old + jnp.dot(rf.astype(bf16), rope, preferred_element_type=f32)) * scale
        old = jnp.where(position < lengths[b], old, -1e30)
        top = jnp.max(old, axis=1, keepdims=True)
        new = []
        for i in range(STEPS):
            fresh_rope = nr[i, b : b + 1, :].astype(f32)
            n = jnp.sum(qf * nl[i, b : b + 1, :].astype(f32), axis=1, keepdims=True)
            n += jnp.sum(rf * jnp.concatenate([fresh_rope, fresh_rope], axis=1), axis=1, keepdims=True)
            n = jnp.where(step_of_row >= i, n * scale, -1e30)
            new.append(n)
            top = jnp.maximum(top, n)
        old = jnp.exp(old - top)
        new = [jnp.exp(n - top) for n in new]
        total = jnp.sum(old, axis=1, keepdims=True) + new[0] + new[1]
        res = jnp.dot((old / total).astype(bf16), cl[b], preferred_element_type=f32)
        for i in range(STEPS):
            res += (new[i] / total).astype(bf16).astype(f32) * nl[i, b : b + 1, :].astype(f32)
        for s in range(STEPS):
            lat[:, s * SLOTS + b, :] = res[s * heads : (s + 1) * heads, :]
    copies[6].wait()
    slot = lax.broadcasted_iota(jnp.int32, (STEPS * SLOTS, HD), 0) % SLOTS
    live = slot < counts[place[0]]
    for h in range(heads):
        ctx = jnp.dot(lat[h].astype(bf16), v[h], preferred_element_type=f32)
        ctx = jnp.where(live, ctx[: STEPS * SLOTS], 0.0).astype(bf16)
        for to in range(NH):
            for s in range(STEPS):
                out[to * 2 + s, :, h * HD : (h + 1) * HD] = ctx[s * SLOTS : (s + 1) * SLOTS]


def attend(place, lengths, counts, *arrays):
    heads = arrays[-1].shape[0]
    scalars = pl.BlockSpec(memory_space=pltpu.SMEM)
    far = pl.BlockSpec(memory_space=pl.ANY)
    return pl.pallas_call(
        attend_kernel,
        in_specs=[scalars] * 3 + [far] * 7,
        out_specs=pl.BlockSpec(memory_space=pltpu.VMEM),
        out_shape=jax.ShapeDtypeStruct((NH * 2, SLOTS, heads * HD), bf16),
        scratch_shapes=[pltpu.VMEM(a.shape, bf16) for a in arrays]
        + [
            pltpu.VMEM((SLOTS, STEPS * heads, LAT), f32),
            pltpu.VMEM((SLOTS, STEPS * heads, 2 * ROPE), f32),
            pltpu.VMEM((heads, 8, LAT), f32),
            pltpu.SemaphoreType.DMA((7,)),
        ],
        cost_estimate=pl.CostEstimate(flops=160_000_000, bytes_accessed=6_000_000, transcendentals=50_000),
    )(place, lengths, counts, *arrays)


def experts_kernel(rows, weight, g0, g1, u0, u1, d0, d1, out):
    parts, chunks = 4, 7
    depth, width = D // parts, D // chunks
    blocks = NXY // parts
    acc = [jnp.zeros((128, 256), f32) for _ in range(2)]
    tot = jnp.zeros((1, 128), f32)
    for i in range(parts):
        k = slice(i * depth, (i + 1) * depth)
        group = slice(i * blocks, (i + 1) * blocks)
        wide = rows[group, : D // 16, :].reshape(depth, 128).T
        for j, (g, u) in enumerate(((g0, u0), (g1, u1))):
            acc[j] += jnp.dot(wide, jnp.concatenate([g[k, :], u[k, :]], axis=1), preferred_element_type=f32)
        tot += jnp.sum(rows[group, D // 16 :, :].astype(f32), axis=(0, 1))[None]
    inv = lax.rsqrt(tot / D + 1e-06).T
    scale = weight[...].T
    inner = []
    for j in range(2):
        gate = acc[j][:, :128] * inv
        up = acc[j][:, 128:] * inv
        inner.append((gate / (1.0 + jnp.exp(-gate)) * up * scale).astype(bf16))
    inner = jnp.concatenate(inner, axis=1)
    for n in range(chunks):
        c = slice(n * width, (n + 1) * width)
        down = jnp.concatenate([d0[:, c], d1[:, c]], axis=0)
        out[:, c] = jnp.dot(inner, down, preferred_element_type=f32).astype(bf16)


def experts(rows, weight, *weights):
    near = pl.BlockSpec(memory_space=pltpu.VMEM)
    return pl.pallas_call(
        experts_kernel,
        in_specs=[near] * 8,
        out_specs=near,
        out_shape=jax.ShapeDtypeStruct((128, D), bf16),
        compiler_params=pltpu.CompilerParams(vmem_limit_bytes=24 * 1024 * 1024),
        cost_estimate=pl.CostEstimate(flops=705_000_000, bytes_accessed=15_000_000, transcendentals=32768),
    )(rows, weight, *weights)


def stage_kernel(a, b, to_a, to_b, sems):
    copies = [pltpu.make_async_copy(a, to_a, sems.at[0]), pltpu.make_async_copy(b, to_b, sems.at[1])]
    for copy in copies:
        copy.start()
    for copy in copies:
        copy.wait()


def stage(*arrays):
    return pl.pallas_call(
        stage_kernel,
        in_specs=[pl.BlockSpec(memory_space=pl.ANY)] * 2,
        out_specs=[pl.BlockSpec(memory_space=pltpu.VMEM)] * 2,
        out_shape=[jax.ShapeDtypeStruct(a.shape, a.dtype) for a in arrays],
        scratch_shapes=[pltpu.SemaphoreType.DMA((2,))],
    )(*arrays)


def unwritten(*arrays):
    return pl.pallas_call(
        lambda *outs: None,
        out_specs=[pl.BlockSpec(memory_space=pltpu.VMEM)] * 2,
        out_shape=[jax.ShapeDtypeStruct(a.shape, a.dtype) for a in arrays],
    )()


def sum_kernel(got, out):
    total = jnp.sum(got[...].astype(f32), axis=0).astype(bf16)
    for h in range(NH):
        for q in range(4):
            out[h * 4 + q] = total[h * SLOTS : (h + 1) * SLOTS, q * (D // 4) : (q + 1) * (D // 4)]


def sum_sources(got):
    near = pl.BlockSpec(memory_space=pltpu.VMEM)
    return pl.pallas_call(
        sum_kernel,
        in_specs=[near],
        out_specs=near,
        out_shape=jax.ShapeDtypeStruct((16, SLOTS, D // 4), bf16),
        compiler_params=pltpu.CompilerParams(vmem_limit_bytes=16 * 1024 * 1024),
    )(got)


def project_kernel(ctx, own, other, out):
    dims = (((1,), (1,)), ((), ()))
    half = own.shape[1]
    part = lax.dot_general(other[...], ctx[:, :half], dims, preferred_element_type=f32)
    part += lax.dot_general(own[...], ctx[:, half:], dims, preferred_element_type=f32)
    part = part.astype(bf16)
    for i in range(NZ):
        out[i] = part


def project(ctx, own, other):
    near = pl.BlockSpec(memory_space=pltpu.VMEM)
    return pl.pallas_call(
        project_kernel,
        in_specs=[near] * 3,
        out_specs=near,
        out_shape=jax.ShapeDtypeStruct((NZ, own.shape[0], 128), bf16),
        compiler_params=pltpu.CompilerParams(vmem_limit_bytes=16 * 1024 * 1024),
    )(ctx, own, other)


def body(
    query_latent,
    query_rope,
    cache_latent,
    cache_rope,
    new_latent,
    new_rope,
    cache_lengths,
    row_counts,
    value_up,
    out_proj,
    norm_gain,
    expert_ids,
    route_gates,
    gate_proj,
    up_proj,
    down_proj,
):
    core = lax.axis_index("c")
    column = lax.axis_index(XY)

    out_other = lax.ppermute(out_proj.T, "c", SWAP)
    gate_other = lax.ppermute(gate_proj, "c", SWAP)
    up_other = lax.ppermute(up_proj, "c", SWAP)
    down_other = lax.ppermute(down_proj, "c", SWAP)

    ctx = attend(
        lax.axis_index(DP)[None],
        cache_lengths,
        row_counts,
        query_latent,
        query_rope,
        cache_latent,
        cache_rope,
        new_latent,
        new_rope,
        value_up,
    )
    ctx = lax.all_to_all(ctx, ("h", "c"), 0, 0).reshape(NH, 2, SLOTS, -1)
    sources = (norm_gain, expert_ids, route_gates, row_counts, up_other, down_other)
    blank = jnp.zeros((D // 16, 128), f32), jnp.zeros((1, 128), f32), *unwritten(up_other, down_other)
    ctx, blank, sources, out_other, gate_other = lax.optimization_barrier(
        (ctx, blank, sources, out_other, gate_other)
    )

    def prepare(norm_gain, expert_ids, route_gates, row_counts, *weights):
        gain = lax.dynamic_slice_in_dim(norm_gain, column * (D // 16), D // 16, 0)
        fours = jnp.sum(jnp.where(expert_ids == column, route_gates, 0.0), axis=2)
        live = (jnp.arange(SLOTS)[None, :] < row_counts[:, None]).astype(f32).reshape(1, 128)
        return (
            jnp.broadcast_to(gain[:, None], (D // 16, 128)),
            lax.dynamic_slice_in_dim(fours, core, 1, 0) * live,
            *stage(*weights),
        )

    early = lax.cond(core == 0, lambda _, sources: prepare(*sources), lambda blank, _: blank, blank, sources)
    ctx, early = lax.optimization_barrier((ctx, early))
    ctx = lax.cond(core == 0, lambda v: jnp.stack([v[:, 1], v[:, 0]], axis=1), lambda v: v, ctx)
    ctx = jnp.transpose(ctx, (0, 2, 1, 3)).reshape(8, -1)
    ctx = spread(ctx, XY, NXY).reshape(128, -1)
    ctx, early, sources = lax.optimization_barrier((ctx, early, sources))
    gain, weight, up_other, down_other = lax.cond(core == 0, lambda early, _: early, lambda _, sources: prepare(*sources), early, sources)

    pieces = lax.all_to_all(project(ctx, out_proj.T, out_other), Z, 0, 0).reshape(NH, 2, D // 64, 128).astype(f32)
    hid = jnp.sum(pieces, axis=1).astype(bf16)
    own_hid = lax.dynamic_index_in_dim(hid, lax.axis_index("h"), 0, keepdims=False)

    hid_f = hid.astype(f32).reshape(D // 16, 128)
    scaled = (hid_f * gain).astype(bf16)
    squares = jnp.sum(hid_f * hid_f, axis=0, keepdims=True)
    high = squares.astype(bf16)
    low = (squares - high.astype(f32)).astype(bf16)
    packed = jnp.concatenate([scaled, high, low, jnp.zeros((14, 128), bf16)], axis=0)
    packed, own_hid = lax.optimization_barrier((packed, own_hid))
    rows = spread(packed, XY, NXY)
    rows, own_hid = lax.optimization_barrier((rows, own_hid))

    out = experts(rows, weight, gate_proj, gate_other, up_proj, up_other, down_proj, down_other)
    out, own_hid = lax.optimization_barrier((out, own_hid))
    got = lax.all_to_all(out.reshape(NXY, 8, D), XY, 0, 0)
    got, own_hid = lax.optimization_barrier((got, own_hid))
    sums = sum_sources(got)

    other_hid = lax.ppermute(own_hid, "c", SWAP)
    steps = jnp.where(core == 0, jnp.stack([own_hid, other_hid]), jnp.stack([other_hid, own_hid]))
    hidden = jnp.transpose(steps, (0, 2, 1))

    own = lax.all_to_all(sums, ("h", "l", "c"), 0, 0)
    mixed = jnp.sum(own.astype(f32).reshape(NZ, STEPS, SLOTS, D // 4), axis=0).astype(bf16)
    return hidden, mixed


def solution(mesh):
    fine = Mesh(mesh.devices.reshape(4, 4, 4, 2, 2), ("x", "y", "h", "l", "c"))
    return jax.shard_map(
        body,
        mesh=fine,
        in_specs=(
            P(None, DP, TP),
            P(None, DP, TP),
            P(DP, None, None),
            P(DP, None, None),
            P(None, DP, None),
            P(None, DP, None),
            P(DP),
            P(),
            P(TP, None, None),
            P(TP, DP),
            P(),
            P(),
            P(),
            P(None, DP + TP),
            P(None, DP + TP),
            P(DP + TP, None),
        ),
        out_specs=(P(None, None, DP), P(None, DP, TP)),
        check_vma=False,
    )
```

```python
import jax
import jax.numpy as jnp
from jax import lax
from jax.experimental import pallas as pl
from jax.experimental.pallas import tpu as pltpu
from jax.sharding import Mesh, PartitionSpec as P

D = 7168
LAT = 512
ROPE = 64
HD = 128
FFN = 2048
STEPS = 2
SLOTS = 2
CACHE = 384

DP = ("x", "y", "h")
TP = ("l", "c")
XY = ("x", "y")
Z = ("h", "l")
NXY = 16
NZ = 8
NH = 4
SWAP = ((0, 1), (1, 0))

bf16 = jnp.bfloat16
f32 = jnp.float32


def spread(value, axes, count):
    copies = jnp.broadcast_to(value[None], (count,) + value.shape)
    return lax.all_to_all(copies, axes, 0, 0)


def attend_kernel(place, lengths, counts, ql_hbm, qr_hbm, cl_hbm, cr_hbm, nl_hbm, nr_hbm, v_hbm, out,
                  ql, qr, cl, cr, nl, nr, v, q_rows, r_rows, lat, sems):
    pairs = ((ql_hbm, ql), (qr_hbm, qr), (cl_hbm, cl), (cr_hbm, cr), (nl_hbm, nl), (nr_hbm, nr), (v_hbm, v))
    copies = [pltpu.make_async_copy(src, dst, sems.at[i]) for i, (src, dst) in enumerate(pairs)]
    for copy in copies:
        copy.start()
    heads = v.shape[0]
    rows = STEPS * heads
    scale = (HD + ROPE) ** (-0.5)
    copies[0].wait()
    copies[1].wait()
    for s in range(STEPS):
        for h in range(heads):
            q_rows[:, s * heads + h, :] = ql[s, :, h * LAT : (h + 1) * LAT].astype(f32)
        for p in range(heads // 2):
            pair = qr[s, :, p * 2 * ROPE : (p + 1) * 2 * ROPE].astype(f32)
            r_rows[:, s * heads + 2 * p, :] = pair
            r_rows[:, s * heads + 2 * p + 1, :] = pair
    for copy in copies[2:6]:
        copy.wait()
    step_of_row = lax.broadcasted_iota(jnp.int32, (rows, 1), 0) // heads
    position = lax.broadcasted_iota(jnp.int32, (rows, CACHE), 1)
    row_id = lax.broadcasted_iota(jnp.int32, (rows, 2 * ROPE), 0)
    lane_id = lax.broadcasted_iota(jnp.int32, (rows, 2 * ROPE), 1)
    own_half = row_id % 2 == lane_id // ROPE
    dims = (((1,), (1,)), ((), ()))
    for b in range(SLOTS):
        qf = q_rows[b]
        rf = jnp.where(own_half, r_rows[b], 0.0)
        rope = jnp.concatenate([cr[b], cr[b]], axis=0)
        old = lax.dot_general(qf.astype(bf16), cl[b], dims, preferred_element_type=f32)
        old = (old + jnp.dot(rf.astype(bf16), rope, preferred_element_type=f32)) * scale
        old = jnp.where(position < lengths[b], old, -1e30)
        top = jnp.max(old, axis=1, keepdims=True)
        new = []
        for i in range(STEPS):
            fresh_rope = nr[i, b : b + 1, :].astype(f32)
            n = jnp.sum(qf * nl[i, b : b + 1, :].astype(f32), axis=1, keepdims=True)
            n += jnp.sum(rf * jnp.concatenate([fresh_rope, fresh_rope], axis=1), axis=1, keepdims=True)
            n = jnp.where(step_of_row >= i, n * scale, -1e30)
            new.append(n)
            top = jnp.maximum(top, n)
        old = jnp.exp(old - top)
        new = [jnp.exp(n - top) for n in new]
        total = jnp.sum(old, axis=1, keepdims=True) + new[0] + new[1]
        res = jnp.dot((old / total).astype(bf16), cl[b], preferred_element_type=f32)
        for i in range(STEPS):
            res += (new[i] / total).astype(bf16).astype(f32) * nl[i, b : b + 1, :].astype(f32)
        for s in range(STEPS):
            lat[:, s * SLOTS + b, :] = res[s * heads : (s + 1) * heads, :]
    copies[6].wait()
    slot = lax.broadcasted_iota(jnp.int32, (STEPS * SLOTS, HD), 0) % SLOTS
    live = slot < counts[place[0]]
    for h in range(heads):
        ctx = jnp.dot(lat[h].astype(bf16), v[h], preferred_element_type=f32)
        ctx = jnp.where(live, ctx[: STEPS * SLOTS], 0.0).astype(bf16)
        for to in range(NH):
            for s in range(STEPS):
                out[to * 2 + s, :, h * HD : (h + 1) * HD] = ctx[s * SLOTS : (s + 1) * SLOTS]


def attend(place, lengths, counts, *arrays):
    heads = arrays[-1].shape[0]
    scalars = pl.BlockSpec(memory_space=pltpu.SMEM)
    far = pl.BlockSpec(memory_space=pl.ANY)
    return pl.pallas_call(
        attend_kernel,
        in_specs=[scalars] * 3 + [far] * 7,
        out_specs=pl.BlockSpec(memory_space=pltpu.VMEM),
        out_shape=jax.ShapeDtypeStruct((NH * 2, SLOTS, heads * HD), bf16),
        scratch_shapes=[pltpu.VMEM(a.shape, bf16) for a in arrays]
        + [
            pltpu.VMEM((SLOTS, STEPS * heads, LAT), f32),
            pltpu.VMEM((SLOTS, STEPS * heads, 2 * ROPE), f32),
            pltpu.VMEM((heads, 8, LAT), f32),
            pltpu.SemaphoreType.DMA((7,)),
        ],
        cost_estimate=pl.CostEstimate(flops=160_000_000, bytes_accessed=6_000_000, transcendentals=50_000),
    )(place, lengths, counts, *arrays)


def experts_kernel(rows, weight, g0, g1, u0, u1, d0, d1, out):
    parts, chunks = 4, 7
    depth, width = D // parts, D // chunks
    blocks = NXY // parts
    acc = [jnp.zeros((128, 256), f32) for _ in range(2)]
    tot = jnp.zeros((1, 128), f32)
    for i in range(parts):
        k = slice(i * depth, (i + 1) * depth)
        group = slice(i * blocks, (i + 1) * blocks)
        wide = rows[group, : D // 16, :].reshape(depth, 128).T
        for j, (g, u) in enumerate(((g0, u0), (g1, u1))):
            acc[j] += jnp.dot(wide, jnp.concatenate([g[k, :], u[k, :]], axis=1), preferred_element_type=f32)
        tot += jnp.sum(rows[group, D // 16 :, :].astype(f32), axis=(0, 1))[None]
    inv = lax.rsqrt(tot / D + 1e-06).T
    scale = weight[...].T
    inner = []
    for j in range(2):
        gate = acc[j][:, :128] * inv
        up = acc[j][:, 128:] * inv
        inner.append((gate / (1.0 + jnp.exp(-gate)) * up * scale).astype(bf16))
    inner = jnp.concatenate(inner, axis=1)
    for n in range(chunks):
        c = slice(n * width, (n + 1) * width)
        down = jnp.concatenate([d0[:, c], d1[:, c]], axis=0)
        out[:, c] = jnp.dot(inner, down, preferred_element_type=f32).astype(bf16)


def experts(rows, weight, *weights):
    near = pl.BlockSpec(memory_space=pltpu.VMEM)
    return pl.pallas_call(
        experts_kernel,
        in_specs=[near] * 8,
        out_specs=near,
        out_shape=jax.ShapeDtypeStruct((128, D), bf16),
        compiler_params=pltpu.CompilerParams(vmem_limit_bytes=24 * 1024 * 1024),
        cost_estimate=pl.CostEstimate(flops=705_000_000, bytes_accessed=15_000_000, transcendentals=32768),
    )(rows, weight, *weights)


def stage_kernel(a, b, to_a, to_b, sems):
    copies = [pltpu.make_async_copy(a, to_a, sems.at[0]), pltpu.make_async_copy(b, to_b, sems.at[1])]
    for copy in copies:
        copy.start()
    for copy in copies:
        copy.wait()


def stage(*arrays):
    return pl.pallas_call(
        stage_kernel,
        in_specs=[pl.BlockSpec(memory_space=pl.ANY)] * 2,
        out_specs=[pl.BlockSpec(memory_space=pltpu.VMEM)] * 2,
        out_shape=[jax.ShapeDtypeStruct(a.shape, a.dtype) for a in arrays],
        scratch_shapes=[pltpu.SemaphoreType.DMA((2,))],
    )(*arrays)


def unwritten(*arrays):
    return pl.pallas_call(
        lambda *outs: None,
        out_specs=[pl.BlockSpec(memory_space=pltpu.VMEM)] * 2,
        out_shape=[jax.ShapeDtypeStruct(a.shape, a.dtype) for a in arrays],
    )()


def sum_kernel(got, out):
    total = jnp.sum(got[...].astype(f32), axis=0).astype(bf16)
    for h in range(NH):
        for q in range(4):
            out[h * 4 + q] = total[h * SLOTS : (h + 1) * SLOTS, q * (D // 4) : (q + 1) * (D // 4)]


def sum_sources(got):
    near = pl.BlockSpec(memory_space=pltpu.VMEM)
    return pl.pallas_call(
        sum_kernel,
        in_specs=[near],
        out_specs=near,
        out_shape=jax.ShapeDtypeStruct((16, SLOTS, D // 4), bf16),
        compiler_params=pltpu.CompilerParams(vmem_limit_bytes=16 * 1024 * 1024),
    )(got)


def finish_kernel(own, out):
    for s in range(STEPS):
        total = own[s].astype(f32)
        for z in range(1, NZ):
            total += own[z * STEPS + s].astype(f32)
        out[s] = total.astype(bf16)


def finish(own):
    near = pl.BlockSpec(memory_space=pltpu.VMEM)
    return pl.pallas_call(
        finish_kernel,
        in_specs=[near],
        out_specs=near,
        out_shape=jax.ShapeDtypeStruct((STEPS, SLOTS, D // 4), bf16),
        compiler_params=pltpu.CompilerParams(vmem_limit_bytes=16 * 1024 * 1024),
    )(own)


def project_kernel(ctx, own, other, out):
    dims = (((1,), (1,)), ((), ()))
    half = own.shape[1]
    part = lax.dot_general(other[...], ctx[:, :half], dims, preferred_element_type=f32)
    part += lax.dot_general(own[...], ctx[:, half:], dims, preferred_element_type=f32)
    part = part.astype(bf16)
    for i in range(NZ):
        out[i] = part


def project(ctx, own, other):
    near = pl.BlockSpec(memory_space=pltpu.VMEM)
    return pl.pallas_call(
        project_kernel,
        in_specs=[near] * 3,
        out_specs=near,
        out_shape=jax.ShapeDtypeStruct((NZ, own.shape[0], 128), bf16),
        compiler_params=pltpu.CompilerParams(vmem_limit_bytes=16 * 1024 * 1024),
    )(ctx, own, other)


def body(
    query_latent,
    query_rope,
    cache_latent,
    cache_rope,
    new_latent,
    new_rope,
    cache_lengths,
    row_counts,
    value_up,
    out_proj,
    norm_gain,
    expert_ids,
    route_gates,
    gate_proj,
    up_proj,
    down_proj,
):
    core = lax.axis_index("c")
    column = lax.axis_index(XY)

    out_other = lax.ppermute(out_proj.T, "c", SWAP)
    gate_other = lax.ppermute(gate_proj, "c", SWAP)
    up_other = lax.ppermute(up_proj, "c", SWAP)
    down_other = lax.ppermute(down_proj, "c", SWAP)

    ctx = attend(
        lax.axis_index(DP)[None],
        cache_lengths,
        row_counts,
        query_latent,
        query_rope,
        cache_latent,
        cache_rope,
        new_latent,
        new_rope,
        value_up,
    )
    ctx = lax.all_to_all(ctx, ("h", "c"), 0, 0).reshape(NH, 2, SLOTS, -1)
    sources = (norm_gain, expert_ids, route_gates, row_counts, up_other, down_other)
    blank = jnp.zeros((D // 16, 128), f32), jnp.zeros((1, 128), f32), *unwritten(up_other, down_other)
    ctx, blank, sources, out_other, gate_other = lax.optimization_barrier(
        (ctx, blank, sources, out_other, gate_other)
    )

    def prepare(norm_gain, expert_ids, route_gates, row_counts, *weights):
        gain = lax.dynamic_slice_in_dim(norm_gain, column * (D // 16), D // 16, 0)
        fours = jnp.sum(jnp.where(expert_ids == column, route_gates, 0.0), axis=2)
        live = (jnp.arange(SLOTS)[None, :] < row_counts[:, None]).astype(f32).reshape(1, 128)
        return (
            jnp.broadcast_to(gain[:, None], (D // 16, 128)),
            lax.dynamic_slice_in_dim(fours, core, 1, 0) * live,
            *stage(*weights),
        )

    early = lax.cond(core == 0, lambda _, sources: prepare(*sources), lambda blank, _: blank, blank, sources)
    ctx, early = lax.optimization_barrier((ctx, early))
    ctx = lax.cond(core == 0, lambda v: jnp.stack([v[:, 1], v[:, 0]], axis=1), lambda v: v, ctx)
    ctx = jnp.transpose(ctx, (0, 2, 1, 3)).reshape(8, -1)
    ctx = spread(ctx, XY, NXY).reshape(128, -1)
    ctx, early, sources = lax.optimization_barrier((ctx, early, sources))
    gain, weight, up_other, down_other = lax.cond(core == 0, lambda early, _: early, lambda _, sources: prepare(*sources), early, sources)

    pieces = lax.all_to_all(project(ctx, out_proj.T, out_other), Z, 0, 0).reshape(NH, 2, D // 64, 128).astype(f32)
    hid = jnp.sum(pieces, axis=1).astype(bf16)
    own_hid = lax.dynamic_index_in_dim(hid, lax.axis_index("h"), 0, keepdims=False)

    hid_f = hid.astype(f32).reshape(D // 16, 128)
    scaled = (hid_f * gain).astype(bf16)
    squares = jnp.sum(hid_f * hid_f, axis=0, keepdims=True)
    high = squares.astype(bf16)
    low = (squares - high.astype(f32)).astype(bf16)
    packed = jnp.concatenate([scaled, high, low, jnp.zeros((14, 128), bf16)], axis=0)
    packed, own_hid = lax.optimization_barrier((packed, own_hid))
    rows = spread(packed, XY, NXY)
    rows, own_hid = lax.optimization_barrier((rows, own_hid))

    out = experts(rows, weight, gate_proj, gate_other, up_proj, up_other, down_proj, down_other)
    out, own_hid = lax.optimization_barrier((out, own_hid))
    got = lax.all_to_all(out.reshape(NXY, 8, D), XY, 0, 0)
    got, own_hid = lax.optimization_barrier((got, own_hid))
    sums = sum_sources(got)

    other_hid = lax.ppermute(own_hid, "c", SWAP)
    steps = jnp.where(core == 0, jnp.stack([own_hid, other_hid]), jnp.stack([other_hid, own_hid]))
    hidden = jnp.transpose(steps, (0, 2, 1))

    own = lax.all_to_all(sums, ("h", "l", "c"), 0, 0)
    mixed = finish(own)
    return hidden, mixed


def solution(mesh):
    fine = Mesh(mesh.devices.reshape(4, 4, 4, 2, 2), ("x", "y", "h", "l", "c"))
    return jax.shard_map(
        body,
        mesh=fine,
        in_specs=(
            P(None, DP, TP),
            P(None, DP, TP),
            P(DP, None, None),
            P(DP, None, None),
            P(None, DP, None),
            P(None, DP, None),
            P(DP),
            P(),
            P(TP, None, None),
            P(TP, DP),
            P(),
            P(),
            P(),
            P(None, DP + TP),
            P(None, DP + TP),
            P(DP + TP, None),
        ),
        out_specs=(P(None, None, DP), P(None, DP, TP)),
        check_vma=False,
    )
```

```python
import jax
import jax.numpy as jnp
from jax import lax
from jax.experimental import pallas as pl
from jax.experimental.pallas import tpu as pltpu
from jax.sharding import Mesh, PartitionSpec as P

D = 7168
LAT = 512
ROPE = 64
HD = 128
FFN = 2048
STEPS = 2
SLOTS = 2
CACHE = 384

DP = ("x", "y", "h")
TP = ("l", "c")
XY = ("x", "y")
Z = ("h", "l")
NXY = 16
NZ = 8
NH = 4
SWAP = ((0, 1), (1, 0))

bf16 = jnp.bfloat16
f32 = jnp.float32


def spread(value, axes, count):
    copies = jnp.broadcast_to(value[None], (count,) + value.shape)
    return lax.all_to_all(copies, axes, 0, 0)


def attend_kernel(place, lengths, counts, ql_hbm, qr_hbm, cl_hbm, cr_hbm, nl_hbm, nr_hbm, v_hbm, out,
                  ql, qr, cl, cr, nl, nr, v, q_rows, r_rows, lat, sems):
    pairs = ((ql_hbm, ql), (qr_hbm, qr), (cl_hbm, cl), (cr_hbm, cr), (nl_hbm, nl), (nr_hbm, nr), (v_hbm, v))
    copies = [pltpu.make_async_copy(src, dst, sems.at[i]) for i, (src, dst) in enumerate(pairs)]
    for copy in copies:
        copy.start()
    heads = v.shape[0]
    rows = STEPS * heads
    scale = (HD + ROPE) ** (-0.5)
    copies[0].wait()
    copies[1].wait()
    for s in range(STEPS):
        for h in range(heads):
            q_rows[:, s * heads + h, :] = ql[s, :, h * LAT : (h + 1) * LAT].astype(f32)
        for p in range(heads // 2):
            pair = qr[s, :, p * 2 * ROPE : (p + 1) * 2 * ROPE].astype(f32)
            r_rows[:, s * heads + 2 * p, :] = pair
            r_rows[:, s * heads + 2 * p + 1, :] = pair
    for copy in copies[2:6]:
        copy.wait()
    step_of_row = lax.broadcasted_iota(jnp.int32, (rows, 1), 0) // heads
    position = lax.broadcasted_iota(jnp.int32, (rows, CACHE), 1)
    row_id = lax.broadcasted_iota(jnp.int32, (rows, 2 * ROPE), 0)
    lane_id = lax.broadcasted_iota(jnp.int32, (rows, 2 * ROPE), 1)
    own_half = row_id % 2 == lane_id // ROPE
    dims = (((1,), (1,)), ((), ()))
    for b in range(SLOTS):
        qf = q_rows[b]
        rf = jnp.where(own_half, r_rows[b], 0.0)
        rope = jnp.concatenate([cr[b], cr[b]], axis=0)
        old = lax.dot_general(qf.astype(bf16), cl[b], dims, preferred_element_type=f32)
        old = (old + jnp.dot(rf.astype(bf16), rope, preferred_element_type=f32)) * scale
        old = jnp.where(position < lengths[b], old, -1e30)
        top = jnp.max(old, axis=1, keepdims=True)
        new = []
        for i in range(STEPS):
            fresh_rope = nr[i, b : b + 1, :].astype(f32)
            n = jnp.sum(qf * nl[i, b : b + 1, :].astype(f32), axis=1, keepdims=True)
            n += jnp.sum(rf * jnp.concatenate([fresh_rope, fresh_rope], axis=1), axis=1, keepdims=True)
            n = jnp.where(step_of_row >= i, n * scale, -1e30)
            new.append(n)
            top = jnp.maximum(top, n)
        old = jnp.exp(old - top)
        new = [jnp.exp(n - top) for n in new]
        total = jnp.sum(old, axis=1, keepdims=True) + new[0] + new[1]
        res = jnp.dot((old / total).astype(bf16), cl[b], preferred_element_type=f32)
        for i in range(STEPS):
            res += (new[i] / total).astype(bf16).astype(f32) * nl[i, b : b + 1, :].astype(f32)
        for s in range(STEPS):
            lat[:, s * SLOTS + b, :] = res[s * heads : (s + 1) * heads, :]
    copies[6].wait()
    slot = lax.broadcasted_iota(jnp.int32, (STEPS * SLOTS, HD), 0) % SLOTS
    live = slot < counts[place[0]]
    for h in range(0, heads, 2):
        rows2 = jnp.concatenate([lat[h], lat[h + 1]], axis=0).astype(bf16)
        both = jnp.dot(rows2, jnp.concatenate([v[h], v[h + 1]], axis=1), preferred_element_type=f32)
        for i in range(2):
            ctx = both[8 * i : 8 * i + STEPS * SLOTS, HD * i : HD * (i + 1)]
            ctx = jnp.where(live, ctx, 0.0).astype(bf16)
            for to in range(NH):
                for s in range(STEPS):
                    out[to * 2 + s, :, (h + i) * HD : (h + i + 1) * HD] = ctx[s * SLOTS : (s + 1) * SLOTS]


def attend(place, lengths, counts, *arrays):
    heads = arrays[-1].shape[0]
    scalars = pl.BlockSpec(memory_space=pltpu.SMEM)
    far = pl.BlockSpec(memory_space=pl.ANY)
    return pl.pallas_call(
        attend_kernel,
        in_specs=[scalars] * 3 + [far] * 7,
        out_specs=pl.BlockSpec(memory_space=pltpu.VMEM),
        out_shape=jax.ShapeDtypeStruct((NH * 2, SLOTS, heads * HD), bf16),
        scratch_shapes=[pltpu.VMEM(a.shape, bf16) for a in arrays]
        + [
            pltpu.VMEM((SLOTS, STEPS * heads, LAT), f32),
            pltpu.VMEM((SLOTS, STEPS * heads, 2 * ROPE), f32),
            pltpu.VMEM((heads, 8, LAT), f32),
            pltpu.SemaphoreType.DMA((7,)),
        ],
        cost_estimate=pl.CostEstimate(flops=160_000_000, bytes_accessed=6_000_000, transcendentals=50_000),
    )(place, lengths, counts, *arrays)


def experts_kernel(rows, weight, g0, g1, u0, u1, d0, d1, out):
    parts, chunks = 4, 7
    depth, width = D // parts, D // chunks
    blocks = NXY // parts
    acc = [jnp.zeros((128, 256), f32) for _ in range(2)]
    tot = jnp.zeros((1, 128), f32)
    for i in range(parts):
        k = slice(i * depth, (i + 1) * depth)
        group = slice(i * blocks, (i + 1) * blocks)
        wide = rows[group, : D // 16, :].reshape(depth, 128).T
        for j, (g, u) in enumerate(((g0, u0), (g1, u1))):
            acc[j] += jnp.dot(wide, jnp.concatenate([g[k, :], u[k, :]], axis=1), preferred_element_type=f32)
        tot += jnp.sum(rows[group, D // 16 :, :].astype(f32), axis=(0, 1))[None]
    inv = lax.rsqrt(tot / D + 1e-06).T
    scale = weight[...].T
    inner = []
    for j in range(2):
        gate = acc[j][:, :128] * inv
        up = acc[j][:, 128:] * inv
        inner.append((gate / (1.0 + jnp.exp(-gate)) * up * scale).astype(bf16))
    inner = jnp.concatenate(inner, axis=1)
    for n in range(chunks):
        c = slice(n * width, (n + 1) * width)
        down = jnp.concatenate([d0[:, c], d1[:, c]], axis=0)
        out[:, c] = jnp.dot(inner, down, preferred_element_type=f32).astype(bf16)


def experts(rows, weight, *weights):
    near = pl.BlockSpec(memory_space=pltpu.VMEM)
    return pl.pallas_call(
        experts_kernel,
        in_specs=[near] * 8,
        out_specs=near,
        out_shape=jax.ShapeDtypeStruct((128, D), bf16),
        compiler_params=pltpu.CompilerParams(vmem_limit_bytes=24 * 1024 * 1024),
        cost_estimate=pl.CostEstimate(flops=705_000_000, bytes_accessed=15_000_000, transcendentals=32768),
    )(rows, weight, *weights)


def stage_kernel(a, b, to_a, to_b, sems):
    copies = [pltpu.make_async_copy(a, to_a, sems.at[0]), pltpu.make_async_copy(b, to_b, sems.at[1])]
    for copy in copies:
        copy.start()
    for copy in copies:
        copy.wait()


def stage(*arrays):
    return pl.pallas_call(
        stage_kernel,
        in_specs=[pl.BlockSpec(memory_space=pl.ANY)] * 2,
        out_specs=[pl.BlockSpec(memory_space=pltpu.VMEM)] * 2,
        out_shape=[jax.ShapeDtypeStruct(a.shape, a.dtype) for a in arrays],
        scratch_shapes=[pltpu.SemaphoreType.DMA((2,))],
    )(*arrays)


def unwritten(*arrays):
    return pl.pallas_call(
        lambda *outs: None,
        out_specs=[pl.BlockSpec(memory_space=pltpu.VMEM)] * 2,
        out_shape=[jax.ShapeDtypeStruct(a.shape, a.dtype) for a in arrays],
    )()


def sum_kernel(got, out):
    total = jnp.sum(got[...].astype(f32), axis=0).astype(bf16)
    for h in range(NH):
        for q in range(4):
            out[h * 4 + q] = total[h * SLOTS : (h + 1) * SLOTS, q * (D // 4) : (q + 1) * (D // 4)]


def sum_sources(got):
    near = pl.BlockSpec(memory_space=pltpu.VMEM)
    return pl.pallas_call(
        sum_kernel,
        in_specs=[near],
        out_specs=near,
        out_shape=jax.ShapeDtypeStruct((16, SLOTS, D // 4), bf16),
        compiler_params=pltpu.CompilerParams(vmem_limit_bytes=16 * 1024 * 1024),
    )(got)


def project_kernel(ctx, own, other, out):
    dims = (((1,), (1,)), ((), ()))
    half = own.shape[1]
    part = lax.dot_general(other[...], ctx[:, :half], dims, preferred_element_type=f32)
    part += lax.dot_general(own[...], ctx[:, half:], dims, preferred_element_type=f32)
    part = part.astype(bf16)
    for i in range(NZ):
        out[i] = part


def project(ctx, own, other):
    near = pl.BlockSpec(memory_space=pltpu.VMEM)
    return pl.pallas_call(
        project_kernel,
        in_specs=[near] * 3,
        out_specs=near,
        out_shape=jax.ShapeDtypeStruct((NZ, own.shape[0], 128), bf16),
        compiler_params=pltpu.CompilerParams(vmem_limit_bytes=16 * 1024 * 1024),
    )(ctx, own, other)


def body(
    query_latent,
    query_rope,
    cache_latent,
    cache_rope,
    new_latent,
    new_rope,
    cache_lengths,
    row_counts,
    value_up,
    out_proj,
    norm_gain,
    expert_ids,
    route_gates,
    gate_proj,
    up_proj,
    down_proj,
):
    core = lax.axis_index("c")
    column = lax.axis_index(XY)

    out_other = lax.ppermute(out_proj.T, "c", SWAP)
    gate_other = lax.ppermute(gate_proj, "c", SWAP)
    up_other = lax.ppermute(up_proj, "c", SWAP)
    down_other = lax.ppermute(down_proj, "c", SWAP)

    ctx = attend(
        lax.axis_index(DP)[None],
        cache_lengths,
        row_counts,
        query_latent,
        query_rope,
        cache_latent,
        cache_rope,
        new_latent,
        new_rope,
        value_up,
    )
    ctx = lax.all_to_all(ctx, ("h", "c"), 0, 0).reshape(NH, 2, SLOTS, -1)
    sources = (norm_gain, expert_ids, route_gates, row_counts, up_other, down_other)
    blank = jnp.zeros((D // 16, 128), f32), jnp.zeros((1, 128), f32), *unwritten(up_other, down_other)
    ctx, blank, sources, out_other, gate_other = lax.optimization_barrier(
        (ctx, blank, sources, out_other, gate_other)
    )

    def prepare(norm_gain, expert_ids, route_gates, row_counts, *weights):
        gain = lax.dynamic_slice_in_dim(norm_gain, column * (D // 16), D // 16, 0)
        fours = jnp.sum(jnp.where(expert_ids == column, route_gates, 0.0), axis=2)
        live = (jnp.arange(SLOTS)[None, :] < row_counts[:, None]).astype(f32).reshape(1, 128)
        return (
            jnp.broadcast_to(gain[:, None], (D // 16, 128)),
            lax.dynamic_slice_in_dim(fours, core, 1, 0) * live,
            *stage(*weights),
        )

    early = lax.cond(core == 0, lambda _, sources: prepare(*sources), lambda blank, _: blank, blank, sources)
    ctx, early = lax.optimization_barrier((ctx, early))
    ctx = lax.cond(core == 0, lambda v: jnp.stack([v[:, 1], v[:, 0]], axis=1), lambda v: v, ctx)
    ctx = jnp.transpose(ctx, (0, 2, 1, 3)).reshape(8, -1)
    ctx = spread(ctx, XY, NXY).reshape(128, -1)
    ctx, early, sources = lax.optimization_barrier((ctx, early, sources))
    gain, weight, up_other, down_other = lax.cond(core == 0, lambda early, _: early, lambda _, sources: prepare(*sources), early, sources)

    pieces = lax.all_to_all(project(ctx, out_proj.T, out_other), Z, 0, 0).reshape(NH, 2, D // 64, 128).astype(f32)
    hid = jnp.sum(pieces, axis=1).astype(bf16)
    own_hid = lax.dynamic_index_in_dim(hid, lax.axis_index("h"), 0, keepdims=False)

    hid_f = hid.astype(f32).reshape(D // 16, 128)
    scaled = (hid_f * gain).astype(bf16)
    squares = jnp.sum(hid_f * hid_f, axis=0, keepdims=True)
    high = squares.astype(bf16)
    low = (squares - high.astype(f32)).astype(bf16)
    packed = jnp.concatenate([scaled, high, low, jnp.zeros((14, 128), bf16)], axis=0)
    packed, own_hid = lax.optimization_barrier((packed, own_hid))
    rows = spread(packed, XY, NXY)
    rows, own_hid = lax.optimization_barrier((rows, own_hid))

    out = experts(rows, weight, gate_proj, gate_other, up_proj, up_other, down_proj, down_other)
    out, own_hid = lax.optimization_barrier((out, own_hid))
    got = lax.all_to_all(out.reshape(NXY, 8, D), XY, 0, 0)
    got, own_hid = lax.optimization_barrier((got, own_hid))
    sums = sum_sources(got)

    other_hid = lax.ppermute(own_hid, "c", SWAP)
    steps = jnp.where(core == 0, jnp.stack([own_hid, other_hid]), jnp.stack([other_hid, own_hid]))
    hidden = jnp.transpose(steps, (0, 2, 1))

    own = lax.all_to_all(sums, ("h", "l", "c"), 0, 0)
    mixed = jnp.sum(own.astype(f32).reshape(NZ, STEPS, SLOTS, D // 4), axis=0).astype(bf16)
    return hidden, mixed


def solution(mesh):
    fine = Mesh(mesh.devices.reshape(4, 4, 4, 2, 2), ("x", "y", "h", "l", "c"))
    return jax.shard_map(
        body,
        mesh=fine,
        in_specs=(
            P(None, DP, TP),
            P(None, DP, TP),
            P(DP, None, None),
            P(DP, None, None),
            P(None, DP, None),
            P(None, DP, None),
            P(DP),
            P(),
            P(TP, None, None),
            P(TP, DP),
            P(),
            P(),
            P(),
            P(None, DP + TP),
            P(None, DP + TP),
            P(DP + TP, None),
        ),
        out_specs=(P(None, None, DP), P(None, DP, TP)),
        check_vma=False,
    )
```
